128 devices in a mesh: rollout: 16 (over y, x), section: 4 (over z), tensor: 2 (over core).
Axes of the slice: x: 4, y: 4, z: 4, core: 2. Of those that a mesh axis runs over, the one named last changes fastest.
Arguments:
- entering: bfloat16 [4, 512, 8192], P('section', 'tensor', 'rollout')
- arriving: bfloat16 [2, 512, 8192], P(None, 'tensor', 'rollout')
- w_query: bfloat16 [4, 8192, 4096], P('section', 'rollout', 'tensor'), may hold values from -0.0625 to 0.0625
- w_keyval: bfloat16 [4, 8192, 2, 1024], P('section', 'rollout', None, 'tensor'), may hold values from -0.0625 to 0.0625
- w_out: bfloat16 [4, 4096, 8192], P('section', 'tensor', 'rollout'), may hold values from -0.75 to 0.75
- query_bias: bfloat16 [4, 4096], P('section', 'tensor')
- keyval_bias: bfloat16 [4, 2, 1024], P('section', None, 'tensor'), may hold values from -3 to 3
- norm_gain: bfloat16 [4, 8192], P('section', 'rollout'), may hold values from 0.5 to 1.5
- resident_kv: bfloat16 [16, 4, 1120, 2, 1024], P('rollout', 'section', None, None, 'tensor')
- resumed_pages: int32 [16], replicated, may hold values from 24 to 32, as said below
- section_active: int32 [4], replicated, may hold values from 0 to 1, as said below
- block_table: int32 [16, 4, 38, 2], replicated, may hold values from 0 to 63, as said below
Outputs:
- section_out: bfloat16 [4, 3, 512, 8192], P('section', None, 'tensor', 'rollout')
- page_pool: bfloat16 [16, 4, 38, 32, 2, 1024], P('rollout', 'section', None, None, None, 'tensor')
The draws below stay inside these ranges and needn't reach their ends.
Inputs may be any that keep to these rules, and one draw needn't show every extreme that they name: `resumed_pages`: some rollout has exactly 32 pages. `section_active`: exactly 3 sections hold a layer. `block_table`: entry [..., 0] names a decode device (rollout index times 4 plus section index) and entry [..., 1] a slot there; every pair of device and slot is named by exactly one page; the 38 pages of each rollout and section name any one decode device at most 1 times, and each of them reaches that bound for some device.
All inputs are finite; a program needn't handle non-finite values.
Results may differ from the reference program's by a relative error of at most 0.029.
Values may be sent and summed in bfloat16 or wider, within the bound.
No kernel may reach another device: no remote copies, remote signals or barrier semaphores. Data moves between devices by JAX's collectives and lax.ppermute only.
A program may use at most 128 MiB of HBM per device.

```python
import functools
import math
import jax
import jax.numpy as jnp
from jax import lax

D = 8192
HQ = 32
KVH = 8
HD = 128
BLOCK = 32
BLOCKS = 3
PAGE = 32
LMAXP = 32
SECTIONS = 4
ROLLOUTS = 16
LAYERS = 3
CTX = 1120
MAXP = 38
DESTS = 64
CAP = 1
N_ROLLOUT = 16
N_TENSOR = 2


def rescale(base, key, rise):
    first, second = jax.random.split(key, 2)
    row_scale = jnp.exp(jax.random.uniform(first, base.shape[:-1] + (1,), jnp.float32, math.log(0.3), math.log(3.0)))
    count = base.shape[-1]
    ramp = jnp.exp((jnp.arange(count, dtype=jnp.float32) / (count - 1) - 0.5) * math.log(rise))
    rough = jnp.exp(jax.random.uniform(second, (count,), jnp.float32, math.log(0.6), math.log(1.6)))
    return (base * row_scale * ramp * rough).astype(jnp.bfloat16)


def draw_entering(key, part):
    key = jax.random.fold_in(key, 21)
    first, second = jax.random.split(key)
    shape = (SECTIONS, ROLLOUTS * BLOCK, D)
    return rescale(jax.random.normal(first, shape, jnp.float32), second, 4.0)


def draw_arriving(key, part):
    key = jax.random.fold_in(key, 22)
    first, second = jax.random.split(key)
    shape = (BLOCKS - 1, ROLLOUTS * BLOCK, D)
    return rescale(jax.random.normal(first, shape, jnp.float32), second, 4.0)


def draw_query_bias(key, part):
    key = jax.random.fold_in(key, 23)
    first = jax.random.fold_in(key, 0)
    noise = jax.random.normal(first, (SECTIONS, HQ, HD), jnp.float32)
    bias = 0.5 * noise
    return bias.reshape(SECTIONS, HQ * HD).astype(jnp.bfloat16)


def draw_resident_kv(key, part):
    key = jax.random.fold_in(key, 24)
    first, second = jax.random.split(key, 2)
    shape = (ROLLOUTS, SECTIONS, CTX, KVH, HD)
    keys = jax.random.normal(first, shape, jnp.float32)
    vals = 1.5 * jax.random.normal(second, shape, jnp.float32)
    return jnp.stack([keys, vals], axis=3).reshape(ROLLOUTS, SECTIONS, CTX, 2, KVH * HD).astype(jnp.bfloat16)


def draw_resumed_pages(key, part):
    key = jax.random.fold_in(key, 31)
    first, second = jax.random.split(key)
    lowest = max(1, 3 * LMAXP // 4)
    pages = jax.random.randint(first, (ROLLOUTS,), lowest, LMAXP + 1)
    chosen = jax.random.randint(second, (), 0, ROLLOUTS)
    return jnp.where(jnp.arange(ROLLOUTS) == chosen, LMAXP, pages).astype(jnp.int32)


def draw_section_active(key, part):
    key = jax.random.fold_in(key, 41)
    order = jax.random.permutation(key, SECTIONS)
    return (order < LAYERS).astype(jnp.int32)


def draw_block_table(key, part):
    key = jax.random.fold_in(key, 51)
    first, second, third, fourth, fifth = jax.random.split(key, 5)
    spots = jax.random.permutation(first, CAP * DESTS)[:MAXP]
    order = jax.random.permutation(second, DESTS)
    placed = jax.random.permutation(third, DESTS)
    turn = jax.random.randint(fourth, (DESTS,), 0, MAXP)
    shuffle = jax.random.permutation(fifth, MAXP)
    residue = (order[:, None] + spots[None, :]) % DESTS
    target = placed[residue]
    slot = (shuffle[None, :] + turn[target]) % MAXP
    return jnp.stack([target, slot], axis=-1).reshape(ROLLOUTS, SECTIONS, MAXP, 2).astype(jnp.int32)


def levels(stream_key, extent, cuts, least, largest):
    def one(position, blocks):
        heights = jax.random.uniform(jax.random.fold_in(jax.random.fold_in(stream_key, 6), position), (blocks,), jnp.float32, least / len(cuts), largest / len(cuts))
        return jnp.repeat(jnp.exp(heights), extent[position] // blocks).reshape((-1,) + (1,) * (len(extent) - position - 1))

    gain = one(*cuts[0])
    for cut in cuts[1:]:
        gain = gain * one(*cut)
    return gain


def scatter_about(stream_key, shape, spread, reach, cuts=(), kind=jnp.bfloat16):
    result = spread * jax.random.normal(stream_key, shape, jnp.float32)
    if cuts:
        result = result * levels(stream_key, shape, cuts, -0.22, 0.18)
    return jnp.clip(result, -reach, reach).astype(kind)


def setup_inputs(seed: int = 0) -> dict:
    seeds = jax.random.split(jax.random.key(seed), 13)
    return {
        "entering": draw_entering(jax.random.fold_in(seeds[12], 71), 0),
        "arriving": draw_arriving(jax.random.fold_in(seeds[12], 71), 0),
        "w_query": scatter_about(seeds[2], (SECTIONS, D, HQ * HD), D ** -0.5, 0.0625, ((0, 4), (1, 16), (2, 2))),
        "w_keyval": scatter_about(seeds[3], (SECTIONS, D, 2, KVH * HD), D ** -0.5, 0.0625, ((0, 4), (1, 16), (3, 2))),
        "w_out": scatter_about(seeds[4], (SECTIONS, HQ * HD, D), (HQ * HD // 64) ** -0.5, 0.75, ((0, 4), (1, 2), (2, 16))),
        "query_bias": draw_query_bias(jax.random.fold_in(seeds[12], 71), 0),
        "keyval_bias": scatter_about(seeds[6], (SECTIONS, 2, KVH * HD), 0.5, 3.0, ((0, 4), (2, 2))),
        "norm_gain": jnp.clip(0.5 + 1.0 * jax.random.uniform(seeds[7], (SECTIONS, D), jnp.float32) ** levels(seeds[7], (SECTIONS, D), ((0, 4), (1, 16)), -0.2, 0.2), 0.5, 1.5).astype(jnp.bfloat16),
        "resident_kv": draw_resident_kv(jax.random.fold_in(seeds[12], 71), 0),
        "resumed_pages": draw_resumed_pages(jax.random.fold_in(seeds[12], 71), 0),
        "section_active": draw_section_active(jax.random.fold_in(seeds[12], 71), 0),
        "block_table": draw_block_table(jax.random.fold_in(seeds[12], 71), 0),
    }


def rotary(values, positions):
    half = HD // 2
    freq = jnp.power(jnp.float32(1000000.0), -(jnp.arange(half, dtype=jnp.float32) * (2.0 / HD)))
    angle = positions.astype(jnp.float32)[:, None] * freq[None, :]
    cosine = jnp.cos(angle)[:, None, :]
    sine = jnp.sin(angle)[:, None, :]
    first = values[..., :half]
    second = values[..., half:]
    return jnp.concatenate([first * cosine - second * sine, second * cosine + first * sine], axis=-1)

def rounded(value):
    return lax.optimization_barrier(value.astype(jnp.bfloat16)).astype(jnp.float32)

def attend(query, cache_keys, cache_vals, new_keys, new_vals, length, step):
    row_count, heads, width = query.shape
    kv_heads = cache_keys.shape[1]
    grouped = query.astype(jnp.float32).reshape(row_count, kv_heads, heads // kv_heads, width)
    scale = 1.0 / math.sqrt(width)
    cached = jnp.einsum('tkgd,jkd->kgtj', grouped, cache_keys.astype(jnp.float32)) * scale
    recent = jnp.einsum('tkgd,jkd->kgtj', grouped, new_keys.astype(jnp.float32)) * scale
    cache_seen = jnp.arange(cache_keys.shape[0], dtype=jnp.int32) < length
    recent_seen = jnp.arange(new_keys.shape[0])[None, :] <= step * row_count + jnp.arange(row_count)[:, None]
    cached = jnp.where(cache_seen, cached, -1e+30)
    recent = jnp.where(recent_seen, recent, -1e+30)
    scores = jnp.concatenate([cached, recent], axis=-1)
    peak = lax.optimization_barrier(jnp.max(scores, axis=-1, keepdims=True))
    powers = jnp.exp(scores - peak)
    weights = (powers / lax.optimization_barrier(jnp.sum(powers, axis=-1, keepdims=True))).astype(jnp.bfloat16)
    values = jnp.concatenate([cache_vals, new_vals], axis=0)
    mixed = jnp.einsum('kgtj,jkd->tkgd', weights.astype(jnp.float32), values.astype(jnp.float32))
    return mixed.reshape(row_count, heads * width).astype(jnp.bfloat16)

def assemble(resident, fresh, start):
    anchor = jnp.zeros((), jnp.int32)
    padded = jnp.concatenate([resident, jnp.zeros_like(fresh)], axis=0)
    padded = lax.dynamic_update_slice(padded, fresh, (start.astype(jnp.int32), anchor, anchor))
    kept_rows = jnp.arange(padded.shape[0], dtype=jnp.int32) < start + fresh.shape[0]
    padded = jnp.where(kept_rows[:, None, None], padded, jnp.zeros_like(padded))
    return padded.reshape(padded.shape[0] // PAGE, PAGE, padded.shape[1], padded.shape[2])

def reference(entering, arriving, w_query, w_keyval, w_out, query_bias, keyval_bias, norm_gain, resident_kv, resumed_pages, section_active, block_table):
    query_width = HQ * HD
    kv_width = KVH * HD
    width_block = D // N_ROLLOUT
    head_group = query_width // N_TENSOR
    token_count = ROLLOUTS * BLOCK
    outputs = [[None] * BLOCKS for _ in range(SECTIONS)]
    fresh_keys = [[] for _ in range(SECTIONS)]
    fresh_vals = [[] for _ in range(SECTIONS)]
    starts = [resumed_pages * PAGE + (SECTIONS - 1 - section) * BLOCK for section in range(SECTIONS)]
    for step in range(BLOCKS):
        for section in range(SECTIONS):
            if step == 0:
                current = entering[section]
            elif section == 0:
                current = arriving[step - 1]
            else:
                current = outputs[section - 1][step - 1]
            xf = current.astype(jnp.float32)
            mean_sq = lax.optimization_barrier(jnp.sum(xf * xf, axis=1, keepdims=True)) / D
            normed = (xf * lax.rsqrt(mean_sq + 1e-06) * norm_gain[section].astype(jnp.float32)).astype(jnp.bfloat16)
            weight_cat = jnp.concatenate([w_query[section], w_keyval[section].reshape(D, 2 * kv_width)], axis=1)
            projected = jnp.zeros((token_count, query_width + 2 * kv_width), jnp.float32)
            for part in range(N_ROLLOUT):
                low = part * width_block
                projected = projected + rounded(jnp.dot(normed[:, low:low + width_block], weight_cat[low:low + width_block], preferred_element_type=jnp.float32))
            query = projected[:, :query_width] + query_bias[section].astype(jnp.float32)
            keys = projected[:, query_width:query_width + kv_width] + keyval_bias[section, 0].astype(jnp.float32)
            vals = projected[:, query_width + kv_width:] + keyval_bias[section, 1].astype(jnp.float32)
            positions = starts[section][:, None] + step * BLOCK + jnp.arange(BLOCK, dtype=jnp.int32)[None, :]
            query = jax.vmap(rotary)(query.reshape(ROLLOUTS, BLOCK, HQ, HD), positions).astype(jnp.bfloat16)
            keys = jax.vmap(rotary)(keys.reshape(ROLLOUTS, BLOCK, KVH, HD), positions).astype(jnp.bfloat16)
            vals = vals.reshape(ROLLOUTS, BLOCK, KVH, HD).astype(jnp.bfloat16)
            fresh_keys[section].append(keys)
            fresh_vals[section].append(vals)
            resident = resident_kv[:, section]
            cache_keys = resident[:, :, 0].reshape(ROLLOUTS, CTX, KVH, HD)
            cache_vals = resident[:, :, 1].reshape(ROLLOUTS, CTX, KVH, HD)
            attended = jax.vmap(functools.partial(attend, step=step))(query, cache_keys, cache_vals, jnp.concatenate(fresh_keys[section], axis=1), jnp.concatenate(fresh_vals[section], axis=1), starts[section])
            attended = attended.reshape(token_count, query_width)
            mixed = jnp.zeros((token_count, D), jnp.float32)
            for part in range(N_TENSOR):
                low = part * head_group
                mixed = mixed + rounded(jnp.dot(attended[:, low:low + head_group], w_out[section, low:low + head_group], preferred_element_type=jnp.float32))
            outputs[section][step] = (xf + section_active[section].astype(jnp.float32) * mixed).astype(jnp.bfloat16)
    pooled = []
    for section in range(SECTIONS):
        fresh = jnp.stack([jnp.concatenate(fresh_keys[section], axis=1).reshape(ROLLOUTS, BLOCKS * BLOCK, kv_width), jnp.concatenate(fresh_vals[section], axis=1).reshape(ROLLOUTS, BLOCKS * BLOCK, kv_width)], axis=2)
        pages = jax.vmap(assemble)(resident_kv[:, section], fresh, starts[section])
        counts = (starts[section] + BLOCKS * BLOCK) // PAGE
        is_live = (jnp.arange(MAXP, dtype=jnp.int32)[None, :] < counts[:, None]) & (section_active[section] > 0)
        pooled.append(jnp.where(is_live[:, :, None, None, None], pages, jnp.zeros_like(pages)))
    pages_all = jnp.stack(pooled, axis=1)
    pool = jnp.zeros((DESTS, MAXP, PAGE, 2, kv_width), jnp.bfloat16)
    pool = pool.at[block_table[..., 0].reshape(-1), block_table[..., 1].reshape(-1)].set(pages_all.reshape(-1, PAGE, 2, kv_width))
    section_out = jnp.stack([jnp.stack(outputs[section]) for section in range(SECTIONS)])
    return (section_out, pool.reshape(ROLLOUTS, SECTIONS, MAXP, PAGE, 2, kv_width))
```

```python
import math

import jax
import jax.numpy as jnp
from jax import lax
from jax.experimental import pallas as pl
from jax.experimental.pallas import tpu as pltpu
from jax.sharding import Mesh, PartitionSpec as P

D = 8192
HD = 128
BLOCK = 32
BLOCKS = 3
PAGE = 32
SIDE = 4
SUMS = 128
ROLL = ("y", "x")
ALL = ("y", "x", "section", "tensor")
F32 = jnp.float32
BF16 = jnp.bfloat16


def dot(a, b):
    return jnp.dot(a, b, preferred_element_type=F32)


def params(*semantics):
    return pltpu.CompilerParams(
        vmem_limit_bytes=56 * 1024 * 1024, dimension_semantics=semantics or None
    )


def ring_routes(phase):
    routes = {}
    for shift in range(1, SIDE):
        route = []
        for y in range(SIDE):
            for x in range(SIDE):
                for s in range(SIDE):
                    for t in range(2):
                        along_x = t == phase
                        ty, tx = (y, (x + shift) % SIDE) if along_x else ((y + shift) % SIDE, x)
                        route.append(
                            (
                                ((y * SIDE + x) * SIDE + s) * 2 + t,
                                ((ty * SIDE + tx) * SIDE + s) * 2 + t,
                            )
                        )
        routes[shift] = route
    return routes


FIRST = ring_routes(0)
SECOND = ring_routes(1)


def ring(block, routes, shift):
    return lax.ppermute(block, ALL, routes[shift])


def split_sum(total):
    high = total.astype(BF16).astype(F32)
    low = total - high
    column = lax.broadcasted_iota(jnp.int32, (total.shape[0], SUMS), 1)
    return jnp.where(column == 0, high, jnp.where(column == 1, low, 0.0)).astype(BF16)


def project_kernel(rows_ref, x_ref, gain_ref, wq_ref, wkv_ref, o0, o1, o2, o3, scaled):
    outs = (o0, o1, o2, o3)
    j = pl.program_id(0)
    query_width = 2048

    @pl.when(j == 0)
    def _():
        gain = gain_ref[...].astype(F32)
        for first in range(SIDE):
            for second in range(SIDE):
                at = pl.multiple_of(rows_ref[first * SIDE + second], BLOCK)
                x = x_ref[pl.ds(at, BLOCK), :].astype(F32)
                low = second * BLOCK
                scaled[first, low : low + BLOCK, :] = (x * gain).astype(BF16)
                squares = jnp.sum(x * x, axis=1, keepdims=True)
                outs[first][low : low + BLOCK, 3072:] = split_sum(squares)

    @pl.when(j < 4)
    def _():
        for first in range(SIDE):
            at = pl.multiple_of(j * 512, 512)
            outs[first][:, pl.ds(at, 512)] = dot(scaled[first], wq_ref[...]).astype(BF16)

    @pl.when(j >= 4)
    def _():
        for first in range(SIDE):
            at = pl.multiple_of(j * 512, 512)
            outs[first][:, pl.ds(at, 512)] = dot(scaled[first], wkv_ref[...]).astype(BF16)


def project(rows, x, gain, wq, wkv):
    depth = x.shape[1]
    tokens = x.shape[0] // SIDE
    width = wq.shape[1] + wkv.shape[1] + SUMS
    whole = pl.BlockSpec((tokens, width), lambda j: (0, 0))
    return pl.pallas_call(
        project_kernel,
        grid=(6,),
        in_specs=[
            pl.BlockSpec(memory_space=pltpu.SMEM),
            pl.BlockSpec(x.shape, lambda j: (0, 0)),
            pl.BlockSpec((1, depth), lambda j: (0, 0)),
            pl.BlockSpec((depth, 512), lambda j: (0, jnp.minimum(j, 3))),
            pl.BlockSpec((depth, 512), lambda j: (0, jnp.maximum(j - 4, 0))),
        ],
        out_specs=[whole] * SIDE,
        out_shape=[jax.ShapeDtypeStruct((tokens, width), BF16)] * SIDE,
        scratch_shapes=[pltpu.VMEM((SIDE, tokens, depth), BF16)],
        compiler_params=params("arbitrary"),
        cost_estimate=pl.CostEstimate(
            flops=2 * x.shape[0] * depth * width, bytes_accessed=7 * 2**20, transcendentals=0
        ),
        name="project",
    )(rows, x, gain, wq, wkv)


def combine_kernel(a_ref, b_ref, c_ref, d_ref, o0, o1, o2, o3):
    outs = (o0, o1, o2, o3)
    last = pl.program_id(0) == pl.num_programs(0) - 1
    for second in range(SIDE):
        at = slice(second * BLOCK, (second + 1) * BLOCK)
        total = (
            a_ref[at, :].astype(F32)
            + b_ref[at, :].astype(F32)
            + c_ref[at, :].astype(F32)
            + d_ref[at, :].astype(F32)
        )
        outs[second][...] = total.astype(BF16)

        @pl.when(last)
        def _():
            squares = jnp.sum(total[:, -SUMS:], axis=1, keepdims=True)
            outs[second][:, total.shape[1] - SUMS :] = split_sum(squares)


def combine(blocks):
    tokens, width = blocks[0].shape
    step = 640
    return pl.pallas_call(
        combine_kernel,
        grid=(width // step,),
        in_specs=[pl.BlockSpec((tokens, step), lambda j: (0, j))] * SIDE,
        out_specs=[pl.BlockSpec((BLOCK, step), lambda j: (0, j))] * SIDE,
        out_shape=[jax.ShapeDtypeStruct((BLOCK, width), BF16)] * SIDE,
        compiler_params=params("arbitrary"),
        cost_estimate=pl.CostEstimate(
            flops=4 * tokens * width, bytes_accessed=10 * tokens * width, transcendentals=0
        ),
        name="combine",
    )(*blocks)


def attend_kernel(step, count, *refs):
    (length_ref, p0, p1, p2, p3, cos_ref, sin_ref, qb_ref, kvb_ref, cache_ref) = refs[:10]
    olds = refs[10 : 10 + 2 * step]
    out_ref, key_ref, val_ref = refs[10 + 2 * step :]
    length = length_ref[0]
    heads = count
    kv_width = heads * HD
    query_width = 4 * kv_width
    parts = (p0, p1, p2, p3)

    def columns(low, high):
        total = parts[0][:, low:high].astype(F32)
        for part in parts[1:]:
            total = total + part[:, low:high].astype(F32)
        return total

    squares = jnp.sum(columns(query_width + 2 * kv_width, p0.shape[1]), axis=1, keepdims=True)
    scale = lax.rsqrt(squares / D + 1e-06)
    cosine = cos_ref[...]
    sine = sin_ref[...]

    def rotate(values):
        return (values * cosine + pltpu.roll(values, HD // 2, 1) * sine).astype(BF16)

    context = cache_ref.shape[0]
    seen = lax.broadcasted_iota(jnp.int32, (1, context), 1) < length
    rows = 4 * BLOCK
    token = lax.broadcasted_iota(jnp.int32, (rows, BLOCK), 0) % BLOCK
    causal = lax.broadcasted_iota(jnp.int32, (rows, BLOCK), 1) <= token
    factor = 1.0 / math.sqrt(HD)

    def scores(q, k):
        return (
            lax.dot_general(q, k, (((1,), (1,)), ((), ())), preferred_element_type=F32) * factor
        )

    for head in range(heads):
        low = head * HD
        key = columns(query_width + low, query_width + low + HD) * scale
        key = rotate(key + kvb_ref[0:1, low : low + HD])
        val = columns(query_width + kv_width + low, query_width + kv_width + low + HD) * scale
        val = (val + kvb_ref[1:2, low : low + HD]).astype(BF16)
        key_ref[:, low : low + HD] = key
        val_ref[:, low : low + HD] = val
        group = []
        for g in range(4):
            at = (head * 4 + g) * HD
            query = columns(at, at + HD) * scale + qb_ref[0:1, at : at + HD]
            group.append(rotate(query))
        query = jnp.concatenate(group, axis=0)
        cached = jnp.where(seen, scores(query, cache_ref[:, low : low + HD]), -1e30)
        recent = [scores(query, olds[2 * i][:, low : low + HD]) for i in range(step)]
        recent.append(jnp.where(causal, scores(query, key), -1e30))
        peak = jnp.max(cached, axis=1, keepdims=True)
        for part in recent:
            peak = jnp.maximum(peak, jnp.max(part, axis=1, keepdims=True))
        powers = jnp.exp(cached - peak)
        total = jnp.sum(powers, axis=1, keepdims=True)
        mixed = dot(powers.astype(BF16), cache_ref[:, kv_width + low : kv_width + low + HD])
        for i, part in enumerate(recent):
            powers = jnp.exp(part - peak)
            total = total + jnp.sum(powers, axis=1, keepdims=True)
            value = olds[2 * i + 1][:, low : low + HD] if i < step else val
            mixed = mixed + dot(powers.astype(BF16), value)
        mixed = (mixed / total).astype(BF16)
        for g in range(4):
            at = (head * 4 + g) * HD
            out_ref[:, at : at + HD] = mixed[g * BLOCK : (g + 1) * BLOCK]


def attend(step, length, parts, cosine, sine, query_bias, keyval_bias, cache, olds):
    kv_width = keyval_bias.shape[1]
    heads = kv_width // HD
    vmem = pl.BlockSpec(memory_space=pltpu.VMEM)
    smem = pl.BlockSpec(memory_space=pltpu.SMEM)
    operands = [*parts, cosine, sine, query_bias, keyval_bias, cache, *olds]
    return pl.pallas_call(
        lambda *refs: attend_kernel(step, heads, *refs),
        in_specs=[smem] + [vmem] * len(operands),
        out_specs=[vmem] * 3,
        out_shape=[
            jax.ShapeDtypeStruct((BLOCK, 4 * kv_width), BF16),
            jax.ShapeDtypeStruct((BLOCK, kv_width), BF16),
            jax.ShapeDtypeStruct((BLOCK, kv_width), BF16),
        ],
        compiler_params=params(),
        cost_estimate=pl.CostEstimate(
            flops=4 * 4 * BLOCK * 1216 * kv_width,
            bytes_accessed=4 * 2**20,
            transcendentals=4 * BLOCK * heads * 1216,
        ),
        name="attend",
    )(length, *operands)


def mix_kernel(rows_ref, a0, a1, a2, a3, w_ref, mine_ref, other_ref, total):
    blocks = (a0, a1, a2, a3)
    k = pl.program_id(0)
    last = k == pl.num_programs(0) - 1
    half = mine_ref.shape[0]
    own = rows_ref[SIDE * SIDE] * half
    for first in range(SIDE):
        product = dot(blocks[first][...], w_ref[...])

        @pl.when(k == 0)
        def _():
            total[first] = product

        @pl.when(k > 0)
        def _():
            total[first] = total[first] + product

        @pl.when(last)
        def _():
            for second in range(SIDE):
                at = rows_ref[first * SIDE + second] - own
                here = (at >= 0) & (at < half)
                value = total[first, second * BLOCK : (second + 1) * BLOCK, :].astype(BF16)

                @pl.when(here)
                def _():
                    mine_ref[pl.ds(pl.multiple_of(at, BLOCK), BLOCK), :] = value

                @pl.when(jnp.logical_not(here))
                def _():
                    there = jnp.where(at < 0, at + half, at - half)
                    other_ref[pl.ds(pl.multiple_of(there, BLOCK), BLOCK), :] = value


def mix(rows, blocks, w):
    tokens, depth = blocks[0].shape
    width = w.shape[1]
    step = 512
    half = pl.BlockSpec((2 * tokens, width), lambda k: (0, 0))
    return pl.pallas_call(
        mix_kernel,
        grid=(depth // step,),
        in_specs=[pl.BlockSpec(memory_space=pltpu.SMEM)]
        + [pl.BlockSpec((tokens, step), lambda k: (0, k))] * SIDE
        + [pl.BlockSpec((step, width), lambda k: (k, 0))],
        out_specs=[half] * 2,
        out_shape=[jax.ShapeDtypeStruct((2 * tokens, width), BF16)] * 2,
        scratch_shapes=[pltpu.VMEM((SIDE, tokens, width), F32)],
        compiler_params=params("arbitrary"),
        cost_estimate=pl.CostEstimate(
            flops=8 * tokens * depth * width, bytes_accessed=5 * 2**20, transcendentals=0
        ),
        name="mix",
    )(rows, *blocks, w)


def ship_kernel(table_ref, resident_ref, f0, f1, f2, out_ref, sems):
    fresh = (f0, f1, f2)
    start = table_ref[38]

    def each(act):
        def body(p, carry):
            @pl.when(p < start)
            def _():
                act(resident_ref.at[p], p)

            return carry

        lax.fori_loop(0, resident_ref.shape[0], body, 0)
        for i in range(BLOCKS):
            act(fresh[i], start + i)

    def begin(source, p):
        pltpu.make_async_copy(source, out_ref.at[table_ref[p]], sems.at[p]).start()

    def end(source, p):
        pltpu.make_async_copy(source, out_ref.at[table_ref[p]], sems.at[p]).wait()

    each(begin)
    each(end)


def ship(table, resident, fresh, count):
    anywhere = pl.BlockSpec(memory_space=pl.ANY)
    return pl.pallas_call(
        ship_kernel,
        in_specs=[pl.BlockSpec(memory_space=pltpu.SMEM)] + [anywhere] * (1 + len(fresh)),
        out_specs=anywhere,
        out_shape=jax.ShapeDtypeStruct((count,) + resident.shape[1:], BF16),
        scratch_shapes=[pltpu.SemaphoreType.DMA((38,))],
        compiler_params=params(),
        cost_estimate=pl.CostEstimate(flops=0, bytes_accessed=5 * 2**20, transcendentals=0),
        name="ship",
    )(table, resident, *fresh)


def store_kernel(table_ref, arrived_ref, pool_ref, blank, sems):
    blank[...] = jnp.zeros_like(blank)

    def each(act):
        def body(q, carry):
            source = table_ref[q]

            @pl.when(source >= 0)
            def _():
                act(arrived_ref.at[jnp.maximum(source, 0)], q)

            @pl.when(source < 0)
            def _():
                act(blank, q)

            return carry

        lax.fori_loop(0, pool_ref.shape[0], body, 0)

    each(lambda source, q: pltpu.make_async_copy(source, pool_ref.at[q], sems.at[q]).start())
    each(lambda source, q: pltpu.make_async_copy(source, pool_ref.at[q], sems.at[q]).wait())


def store(table, arrived, slots):
    anywhere = pl.BlockSpec(memory_space=pl.ANY)
    return pl.pallas_call(
        store_kernel,
        in_specs=[pl.BlockSpec(memory_space=pltpu.SMEM), anywhere],
        out_specs=anywhere,
        out_shape=jax.ShapeDtypeStruct((slots,) + arrived.shape[1:], BF16),
        scratch_shapes=[
            pltpu.VMEM(arrived.shape[1:], BF16),
            pltpu.SemaphoreType.DMA((slots,)),
        ],
        compiler_params=params(),
        cost_estimate=pl.CostEstimate(flops=0, bytes_accessed=5 * 2**20, transcendentals=0),
        name="store",
    )(table, arrived)


def local(
    entering,
    arriving,
    w_query,
    w_keyval,
    w_out,
    query_bias,
    keyval_bias,
    norm_gain,
    resident_kv,
    resumed_pages,
    section_active,
    block_table,
):
    section_count = lax.axis_size("section")
    y = lax.axis_index("y")
    x = lax.axis_index("x")
    section = lax.axis_index("section")
    tensor = lax.axis_index("tensor")
    rollout = y * SIDE + x
    roll_count = SIDE * SIDE
    kv_width = w_keyval.shape[3]
    wq = w_query[0]
    wkv = w_keyval[0].reshape(w_keyval.shape[1], 2 * kv_width)
    w_mix = w_out[0]
    length = resumed_pages[rollout] * PAGE + (section_count - 1 - section) * BLOCK
    active = section_active[section].astype(F32)

    first = jnp.arange(SIDE, dtype=jnp.int32)[:, None]
    second = jnp.arange(SIDE, dtype=jnp.int32)[None, :]
    by_x = ((second + y) % SIDE) * SIDE + (first + x) % SIDE
    by_y = ((first + y) % SIDE) * SIDE + (second + x) % SIDE
    rows = (jnp.where(tensor == 0, by_x, by_y) * BLOCK).reshape(-1)
    rows = jnp.concatenate([rows, tensor[None]]).astype(jnp.int32)

    half = HD // 2
    freq = jnp.power(F32(1000000.0), -(jnp.arange(half, dtype=F32) * (2.0 / HD)))
    positions = length + jnp.arange(BLOCKS * BLOCK, dtype=jnp.int32)
    angle = positions.astype(F32)[:, None] * freq[None, :]
    cosine = jnp.concatenate([jnp.cos(angle), jnp.cos(angle)], axis=1)
    sine = jnp.concatenate([-jnp.sin(angle), jnp.sin(angle)], axis=1)

    resident = resident_kv[0, 0]
    cache = resident.reshape(resident.shape[0], 2 * kv_width)
    query_shift = query_bias.astype(F32)
    keyval_shift = keyval_bias[0].astype(F32)
    swap = [(0, 1), (1, 0)]
    relay = [(i, i + 1) for i in range(section_count - 1)]

    results = []
    olds = []
    current = entering[0]
    for step in range(BLOCKS):
        if step > 0:
            handed = lax.ppermute(results[-1], "section", relay)
            current = jnp.where(section == 0, arriving[step - 1], handed)
        whole = lax.all_gather(current, "tensor", axis=0, tiled=True)
        outs = project(rows, whole, norm_gain, wq, wkv)
        parts = [outs[0]] + [ring(outs[d], FIRST, d) for d in (2, 1, 3)]
        outs = combine(parts)
        parts = [outs[0]] + [ring(outs[d], SECOND, d) for d in (2, 1, 3)]
        at = step * BLOCK
        attended, key, val = attend(
            step,
            length[None],
            parts,
            cosine[at : at + BLOCK],
            sine[at : at + BLOCK],
            query_shift,
            keyval_shift,
            cache,
            olds,
        )
        olds += [key, val]
        gathered = jnp.concatenate(
            [attended] + [ring(attended, SECOND, (SIDE - d) % SIDE) for d in range(1, SIDE)]
        )
        blocks = [gathered] + [ring(gathered, FIRST, (SIDE - d) % SIDE) for d in range(1, SIDE)]
        mine, other = mix(rows, blocks, w_mix)
        theirs = lax.ppermute(other, "tensor", swap)
        summed = mine.astype(F32) + theirs.astype(F32)
        results.append((current.astype(F32) + active * summed).astype(BF16))
    section_out = jnp.stack(results)[None]

    dest_count = roll_count * section_count
    slots = block_table.shape[2]
    routing = block_table.reshape(dest_count, slots, 2)
    targets = routing[:, :, 0]
    slot_ids = routing[:, :, 1]
    own = rollout * section_count + section
    sources = jnp.arange(dest_count, dtype=jnp.int32)
    source_pages = (
        resumed_pages[:, None]
        + (section_count - 1 - jnp.arange(section_count, dtype=jnp.int32))[None, :]
        + BLOCKS
    )
    live_pages = jnp.where(section_active[None, :] > 0, source_pages, 0).reshape(-1)
    page_ids = jnp.arange(slots, dtype=jnp.int32)
    mine = (targets == own) & (page_ids[None, :] < live_pages[:, None])
    hit = mine[:, :, None] & (slot_ids[:, :, None] == page_ids)
    origin = jnp.max(jnp.where(hit, sources[:, None, None], -1), axis=(0, 1))
    sending = jnp.concatenate([targets[own], (length // PAGE)[None]]).astype(jnp.int32)

    pages = resident.reshape(-1, PAGE, 2, kv_width)
    fresh = [jnp.stack([olds[2 * i], olds[2 * i + 1]], axis=1) for i in range(BLOCKS)]
    outgoing = ship(sending, pages, fresh, dest_count)
    arrived = lax.all_to_all(outgoing, ROLL + ("section",), 0, 0, tiled=True)
    pool = store(origin, arrived, slots)
    return section_out, pool[None, None]


def solution(mesh):
    split = Mesh(mesh.devices.reshape(SIDE, SIDE, mesh.shape["section"], 2), ALL)
    in_specs = (
        P("section", "tensor", ROLL),
        P(None, "tensor", ROLL),
        P("section", ROLL, "tensor"),
        P("section", ROLL, None, "tensor"),
        P("section", "tensor", ROLL),
        P("section", "tensor"),
        P("section", None, "tensor"),
        P("section", ROLL),
        P(ROLL, "section", None, None, "tensor"),
        P(),
        P(),
        P(),
    )
    out_specs = (
        P("section", None, "tensor", ROLL),
        P(ROLL, "section", None, None, None, "tensor"),
    )
    return jax.shard_map(
        local, mesh=split, in_specs=in_specs, out_specs=out_specs, check_vma=False
    )
```

```python
import math

import jax
import jax.numpy as jnp
from jax import lax
from jax.experimental import pallas as pl
from jax.experimental.pallas import tpu as pltpu
from jax.sharding import Mesh, PartitionSpec as P

D = 8192
HD = 128
BLOCK = 32
BLOCKS = 3
PAGE = 32
SIDE = 4
SUMS = 128
ROLL = ("y", "x")
ALL = ("y", "x", "section", "tensor")
F32 = jnp.float32
BF16 = jnp.bfloat16


def dot(a, b):
    return jnp.dot(a, b, preferred_element_type=F32)


def params(megabytes):
    return pltpu.CompilerParams(vmem_limit_bytes=megabytes * 1024 * 1024)


def ring_routes(phase):
    routes = {}
    for shift in range(1, SIDE):
        route = []
        for y in range(SIDE):
            for x in range(SIDE):
                for s in range(SIDE):
                    for t in range(2):
                        along_x = t == phase
                        ty, tx = (y, (x + shift) % SIDE) if along_x else ((y + shift) % SIDE, x)
                        route.append(
                            (
                                ((y * SIDE + x) * SIDE + s) * 2 + t,
                                ((ty * SIDE + tx) * SIDE + s) * 2 + t,
                            )
                        )
        routes[shift] = route
    return routes


FIRST = ring_routes(0)
SECOND = ring_routes(1)


def ring(block, routes, shift):
    return lax.ppermute(block, ALL, routes[shift])


ORDER = (2, 1, 3, 0)
CHUNK = 1024


def fetch(wq_ref, wkv_ref, held, sems):
    copies = []
    for i in range(wq_ref.shape[1] // CHUNK):
        part = wq_ref.at[:, pl.ds(i * CHUNK, CHUNK)]
        copies.append(pltpu.make_async_copy(part, held.at[i], sems.at[i]))
    copies.append(pltpu.make_async_copy(wkv_ref, held.at[len(copies)], sems.at[len(copies)]))
    for copy in copies:
        copy.start()
    return copies


def lead_kernel(rows_ref, x_ref, gain_ref, wq_ref, wkv_ref, out, scaled, squares, held, sems):
    copies = fetch(wq_ref, wkv_ref, held, sems)
    count = x_ref.shape[0] // (SIDE * SIDE)
    depth = x_ref.shape[1]
    width = CHUNK * len(copies)
    gain = gain_ref[...].astype(F32)
    lead = []
    for n, first in enumerate(ORDER):
        for second in range(SIDE):
            at = pl.multiple_of(rows_ref[first * SIDE + second] * count, count)
            x = x_ref[pl.ds(at, count), :].astype(F32)
            square = x * x
            sums = square[:, :SUMS]
            for low in range(SUMS, depth, SUMS):
                sums = sums + square[:, low : low + SUMS]
            value = (x * gain).astype(BF16)
            if n == 0:
                lead.append(value)
                out[second * count : (second + 1) * count, width:] = sums.astype(BF16)
            else:
                low = ((n - 1) * SIDE + second) * count
                scaled[low : low + count, :] = value
                squares[low : low + count, :] = sums.astype(BF16)
    lead = jnp.concatenate(lead, axis=0)
    for i, copy in enumerate(copies):
        copy.wait()
        out[:, i * CHUNK : (i + 1) * CHUNK] = dot(lead, held[i]).astype(BF16)


def rest_kernel(scaled, squares, wq_ref, wkv_ref, o1, o3, o0, held, sems):
    copies = fetch(wq_ref, wkv_ref, held, sems)
    tokens = o0.shape[0]
    width = CHUNK * len(copies)
    value = scaled[...]
    for n, out in enumerate((o1, o3, o0)):
        out[:, width:] = squares[n * tokens : (n + 1) * tokens, :]
    for i, copy in enumerate(copies):
        copy.wait()
        product = dot(value, held[i]).astype(BF16)
        for n, out in enumerate((o1, o3, o0)):
            out[:, i * CHUNK : (i + 1) * CHUNK] = product[n * tokens : (n + 1) * tokens]


def project(rows, x, gain, wq, wkv):
    depth = x.shape[1]
    tokens = x.shape[0] // SIDE
    inner = wq.shape[1] + wkv.shape[1]
    chunks = inner // CHUNK
    vmem = pl.BlockSpec(memory_space=pltpu.VMEM)
    smem = pl.BlockSpec(memory_space=pltpu.SMEM)
    anywhere = pl.BlockSpec(memory_space=pl.ANY)
    block = jax.ShapeDtypeStruct((tokens, inner + SUMS), BF16)
    scratch = [pltpu.VMEM((chunks, depth, CHUNK), BF16), pltpu.SemaphoreType.DMA((chunks,))]
    flops = 2 * tokens * depth * inner
    o2, scaled, squares = pl.pallas_call(
        lead_kernel,
        in_specs=[smem, vmem, vmem, anywhere, anywhere],
        out_specs=[vmem] * 3,
        out_shape=[
            block,
            jax.ShapeDtypeStruct((3 * tokens, depth), BF16),
            jax.ShapeDtypeStruct((3 * tokens, SUMS), BF16),
        ],
        scratch_shapes=scratch,
        compiler_params=params(14),
        cost_estimate=pl.CostEstimate(
            flops=flops, bytes_accessed=6 * 2**20, transcendentals=0
        ),
        name="project_lead",
    )(rows, x, gain, wq, wkv)
    o1, o3, o0 = pl.pallas_call(
        rest_kernel,
        in_specs=[vmem, vmem, anywhere, anywhere],
        out_specs=[vmem] * 3,
        out_shape=[block] * 3,
        scratch_shapes=scratch,
        compiler_params=params(14),
        cost_estimate=pl.CostEstimate(
            flops=3 * flops, bytes_accessed=6 * 2**20, transcendentals=0
        ),
        name="project_rest",
    )(scaled, squares, wq, wkv)
    return o0, o1, o2, o3


def combine(blocks):
    count = blocks[0].shape[0] // SIDE
    outs = []
    for second in range(SIDE):
        at = slice(second * count, (second + 1) * count)
        total = blocks[0][at].astype(F32)
        for block in blocks[1:]:
            total = total + block[at].astype(F32)
        outs.append(total.astype(BF16))
    return outs


def attend_kernel(step, count, *refs):
    (length_ref, p0, p1, p2, p3, cos_ref, sin_ref, qb_ref, kvb_ref, cache_ref) = refs[:10]
    olds = refs[10 : 10 + 2 * step]
    out_ref, key_ref, val_ref, held, sems = refs[10 + 2 * step :]
    length = length_ref[0]
    heads = count
    copies = []
    for head in range(heads):
        for kind in range(2):
            part = cache_ref.at[:, pl.ds((kind * heads + head) * HD, HD)]
            at = 2 * head + kind
            copies.append(pltpu.make_async_copy(part, held.at[at], sems.at[at]))
            copies[-1].start()
    kv_width = heads * HD
    query_width = 4 * kv_width
    parts = (p0, p1, p2, p3)

    def columns(low, high):
        total = parts[0][:, low:high].astype(F32)
        for part in parts[1:]:
            total = total + part[:, low:high].astype(F32)
        return total

    squares = jnp.sum(columns(query_width + 2 * kv_width, p0.shape[1]), axis=1, keepdims=True)
    scale = lax.rsqrt(squares / D + 1e-06)
    cosine = cos_ref[...]
    sine = sin_ref[...]

    def rotate(values):
        return (values * cosine + pltpu.roll(values, HD // 2, 1) * sine).astype(BF16)

    context = cache_ref.shape[0]
    seen = lax.broadcasted_iota(jnp.int32, (1, context), 1) < length
    rows = 4 * BLOCK
    token = lax.broadcasted_iota(jnp.int32, (rows, BLOCK), 0) % BLOCK
    causal = lax.broadcasted_iota(jnp.int32, (rows, BLOCK), 1) <= token
    factor = 1.0 / math.sqrt(HD)

    def scores(q, k):
        return (
            lax.dot_general(q, k, (((1,), (1,)), ((), ())), preferred_element_type=F32) * factor
        )

    for head in range(heads):
        low = head * HD
        key = columns(query_width + low, query_width + low + HD) * scale
        key = rotate(key + kvb_ref[0:1, low : low + HD])
        val = columns(query_width + kv_width + low, query_width + kv_width + low + HD) * scale
        val = (val + kvb_ref[1:2, low : low + HD]).astype(BF16)
        key_ref[:, low : low + HD] = key
        val_ref[:, low : low + HD] = val
        group = []
        for g in range(4):
            at = (head * 4 + g) * HD
            query = columns(at, at + HD) * scale + qb_ref[0:1, at : at + HD]
            group.append(rotate(query))
        query = jnp.concatenate(group, axis=0)
        copies[2 * head].wait()
        cached = jnp.where(seen, scores(query, held[2 * head]), -1e30)
        recent = [scores(query, olds[2 * i][:, low : low + HD]) for i in range(step)]
        recent.append(jnp.where(causal, scores(query, key), -1e30))
        peak = jnp.max(cached, axis=1, keepdims=True)
        for part in recent:
            peak = jnp.maximum(peak, jnp.max(part, axis=1, keepdims=True))
        powers = jnp.exp(cached - peak)
        total = jnp.sum(powers, axis=1, keepdims=True)
        copies[2 * head + 1].wait()
        mixed = dot(powers.astype(BF16), held[2 * head + 1])
        for i, part in enumerate(recent):
            powers = jnp.exp(part - peak)
            total = total + jnp.sum(powers, axis=1, keepdims=True)
            value = olds[2 * i + 1][:, low : low + HD] if i < step else val
            mixed = mixed + dot(powers.astype(BF16), value)
        mixed = (mixed / total).astype(BF16)
        for g in range(4):
            at = (head * 4 + g) * HD
            out_ref[:, at : at + HD] = mixed[g * BLOCK : (g + 1) * BLOCK]


def attend(step, length, parts, cosine, sine, query_bias, keyval_bias, cache, olds):
    kv_width = keyval_bias.shape[1]
    heads = kv_width // HD
    vmem = pl.BlockSpec(memory_space=pltpu.VMEM)
    smem = pl.BlockSpec(memory_space=pltpu.SMEM)
    anywhere = pl.BlockSpec(memory_space=pl.ANY)
    operands = [*parts, cosine, sine, query_bias, keyval_bias, cache, *olds]
    in_specs = [smem] + [vmem] * 8 + [anywhere] + [vmem] * len(olds)
    return pl.pallas_call(
        lambda *refs: attend_kernel(step, heads, *refs),
        in_specs=in_specs,
        out_specs=[vmem] * 3,
        out_shape=[
            jax.ShapeDtypeStruct((BLOCK, 4 * kv_width), BF16),
            jax.ShapeDtypeStruct((BLOCK, kv_width), BF16),
            jax.ShapeDtypeStruct((BLOCK, kv_width), BF16),
        ],
        scratch_shapes=[
            pltpu.VMEM((2 * heads, cache.shape[0], HD), BF16),
            pltpu.SemaphoreType.DMA((2 * heads,)),
        ],
        compiler_params=params(16),
        cost_estimate=pl.CostEstimate(
            flops=4 * 4 * BLOCK * 1216 * kv_width,
            bytes_accessed=4 * 2**20,
            transcendentals=4 * BLOCK * heads * 1216,
        ),
        name="attend",
    )(length, *operands)


def place_kernel(rows_ref, p0, p1, p2, p3, mine_ref, other_ref):
    half = mine_ref.shape[0]
    count = p0.shape[0] // SIDE
    own = rows_ref[SIDE * SIDE] * half
    for first, block in enumerate((p0, p1, p2, p3)):
        for second in range(SIDE):
            at = rows_ref[first * SIDE + second] * count - own
            here = (at >= 0) & (at < half)
            value = block[second * count : (second + 1) * count, :]

            @pl.when(here)
            def _():
                mine_ref[pl.ds(pl.multiple_of(at, count), count), :] = value

            @pl.when(jnp.logical_not(here))
            def _():
                there = jnp.where(at < 0, at + half, at - half)
                other_ref[pl.ds(pl.multiple_of(there, count), count), :] = value


def place(rows, blocks):
    tokens, width = blocks[0].shape
    vmem = pl.BlockSpec(memory_space=pltpu.VMEM)
    return pl.pallas_call(
        place_kernel,
        in_specs=[pl.BlockSpec(memory_space=pltpu.SMEM)] + [vmem] * SIDE,
        out_specs=[vmem] * 2,
        out_shape=[jax.ShapeDtypeStruct((2 * tokens, width), BF16)] * 2,
        compiler_params=params(8),
        cost_estimate=pl.CostEstimate(flops=0, bytes_accessed=2**20, transcendentals=0),
        name="place",
    )(rows, *blocks)


def ship_kernel(table_ref, resident_ref, f0, f1, f2, out_ref, sems):
    fresh = (f0, f1, f2)
    start = table_ref[38]

    def each(act):
        def body(p, carry):
            @pl.when(p < start)
            def _():
                act(resident_ref.at[p], p)

            return carry

        lax.fori_loop(0, resident_ref.shape[0], body, 0)
        for i in range(BLOCKS):
            act(fresh[i], start + i)

    def begin(source, p):
        pltpu.make_async_copy(source, out_ref.at[table_ref[p]], sems.at[p]).start()

    def end(source, p):
        pltpu.make_async_copy(source, out_ref.at[table_ref[p]], sems.at[p]).wait()

    each(begin)
    each(end)


def ship(table, resident, fresh, count):
    anywhere = pl.BlockSpec(memory_space=pl.ANY)
    return pl.pallas_call(
        ship_kernel,
        in_specs=[pl.BlockSpec(memory_space=pltpu.SMEM)] + [anywhere] * (1 + len(fresh)),
        out_specs=anywhere,
        out_shape=jax.ShapeDtypeStruct((count,) + resident.shape[1:], BF16),
        scratch_shapes=[pltpu.SemaphoreType.DMA((38,))],
        compiler_params=params(4),
        cost_estimate=pl.CostEstimate(flops=0, bytes_accessed=5 * 2**20, transcendentals=0),
        name="ship",
    )(table, resident, *fresh)


def store_kernel(table_ref, arrived_ref, pool_ref, blank, sems):
    blank[...] = jnp.zeros_like(blank)

    def each(act):
        def body(q, carry):
            source = table_ref[q]

            @pl.when(source >= 0)
            def _():
                act(arrived_ref.at[jnp.maximum(source, 0)], q)

            @pl.when(source < 0)
            def _():
                act(blank, q)

            return carry

        lax.fori_loop(0, pool_ref.shape[0], body, 0)

    each(lambda source, q: pltpu.make_async_copy(source, pool_ref.at[q], sems.at[q]).start())
    each(lambda source, q: pltpu.make_async_copy(source, pool_ref.at[q], sems.at[q]).wait())


def store(table, arrived, slots):
    anywhere = pl.BlockSpec(memory_space=pl.ANY)
    return pl.pallas_call(
        store_kernel,
        in_specs=[pl.BlockSpec(memory_space=pltpu.SMEM), anywhere],
        out_specs=anywhere,
        out_shape=jax.ShapeDtypeStruct((slots,) + arrived.shape[1:], BF16),
        scratch_shapes=[
            pltpu.VMEM(arrived.shape[1:], BF16),
            pltpu.SemaphoreType.DMA((slots,)),
        ],
        compiler_params=params(4),
        cost_estimate=pl.CostEstimate(flops=0, bytes_accessed=5 * 2**20, transcendentals=0),
        name="store",
    )(table, arrived)


def local(
    entering,
    arriving,
    w_query,
    w_keyval,
    w_out,
    query_bias,
    keyval_bias,
    norm_gain,
    resident_kv,
    resumed_pages,
    section_active,
    block_table,
):
    section_count = lax.axis_size("section")
    y = lax.axis_index("y")
    x = lax.axis_index("x")
    section = lax.axis_index("section")
    tensor = lax.axis_index("tensor")
    rollout = y * SIDE + x
    roll_count = SIDE * SIDE
    kv_width = w_keyval.shape[3]
    wq = w_query[0]
    wkv = w_keyval[0].reshape(w_keyval.shape[1], 2 * kv_width)
    w_mix = w_out[0]
    length = resumed_pages[rollout] * PAGE + (section_count - 1 - section) * BLOCK
    active = section_active[section].astype(F32)

    first = jnp.arange(SIDE, dtype=jnp.int32)[:, None]
    second = jnp.arange(SIDE, dtype=jnp.int32)[None, :]
    by_x = ((second + y) % SIDE) * SIDE + (first + x) % SIDE
    by_y = ((first + y) % SIDE) * SIDE + (second + x) % SIDE
    rows = jnp.where(tensor == 0, by_x, by_y).reshape(-1)
    rows = jnp.concatenate([rows, tensor[None]]).astype(jnp.int32)

    half = HD // 2
    freq = jnp.power(F32(1000000.0), -(jnp.arange(half, dtype=F32) * (2.0 / HD)))
    positions = length + jnp.arange(BLOCKS * BLOCK, dtype=jnp.int32)
    angle = positions.astype(F32)[:, None] * freq[None, :]
    cosine = jnp.concatenate([jnp.cos(angle), jnp.cos(angle)], axis=1)
    sine = jnp.concatenate([-jnp.sin(angle), jnp.sin(angle)], axis=1)

    resident = resident_kv[0, 0]
    cache = resident.reshape(resident.shape[0], 2 * kv_width)
    query_shift = query_bias.astype(F32)
    keyval_shift = keyval_bias[0].astype(F32)
    swap = [(0, 1), (1, 0)]
    relay = [(i, i + 1) for i in range(section_count - 1)]

    results = []
    olds = []
    current = entering[0]
    for step in range(BLOCKS):
        if step > 0:
            handed = lax.ppermute(results[-1], "section", relay)
            current = jnp.where(section == 0, arriving[step - 1], handed)
        whole = lax.all_gather(current, "tensor", axis=0, tiled=True)
        outs = project(rows, whole, norm_gain, wq, wkv)
        parts = [outs[0]] + [ring(outs[d], FIRST, d) for d in (2, 1, 3)]
        outs = combine(parts)
        parts = [outs[0]] + [ring(outs[d], SECOND, d) for d in (2, 1, 3)]
        at = step * BLOCK
        attended, key, val = attend(
            step,
            length[None],
            parts,
            cosine[at : at + BLOCK],
            sine[at : at + BLOCK],
            query_shift,
            keyval_shift,
            cache,
            olds,
        )
        olds += [key, val]
        gathered = jnp.concatenate(
            [attended] + [ring(attended, SECOND, (SIDE - d) % SIDE) for d in range(1, SIDE)]
        )
        blocks = [gathered] + [ring(gathered, FIRST, (SIDE - d) % SIDE) for d in range(1, SIDE)]
        mine, other = place(rows, [dot(block, w_mix).astype(BF16) for block in blocks])
        theirs = lax.ppermute(other, "tensor", swap)
        summed = mine.astype(F32) + theirs.astype(F32)
        results.append((current.astype(F32) + active * summed).astype(BF16))
    section_out = jnp.stack(results)[None]

    dest_count = roll_count * section_count
    slots = block_table.shape[2]
    routing = block_table.reshape(dest_count, slots, 2)
    targets = routing[:, :, 0]
    slot_ids = routing[:, :, 1]
    own = rollout * section_count + section
    sources = jnp.arange(dest_count, dtype=jnp.int32)
    source_pages = (
        resumed_pages[:, None]
        + (section_count - 1 - jnp.arange(section_count, dtype=jnp.int32))[None, :]
        + BLOCKS
    )
    live_pages = jnp.where(section_active[None, :] > 0, source_pages, 0).reshape(-1)
    page_ids = jnp.arange(slots, dtype=jnp.int32)
    mine = (targets == own) & (page_ids[None, :] < live_pages[:, None])
    hit = mine[:, :, None] & (slot_ids[:, :, None] == page_ids)
    origin = jnp.max(jnp.where(hit, sources[:, None, None], -1), axis=(0, 1))
    sending = jnp.concatenate([targets[own], (length // PAGE)[None]]).astype(jnp.int32)

    heads = kv_width // HD
    pages = resident.reshape(-1, 2, heads, HD).swapaxes(1, 2).reshape(-1, PAGE * 2 * heads, HD)
    fresh = [
        jnp.stack(
            [olds[2 * i].reshape(PAGE, heads, HD), olds[2 * i + 1].reshape(PAGE, heads, HD)],
            axis=2,
        ).reshape(PAGE * 2 * heads, HD)
        for i in range(BLOCKS)
    ]
    outgoing = ship(sending, pages, fresh, dest_count)
    arrived = lax.all_to_all(outgoing, ROLL + ("section",), 0, 0, tiled=True)
    pool = store(origin, arrived, slots)
    pool = pool.reshape(slots * PAGE, heads, 2, HD).swapaxes(1, 2)
    return section_out, pool.reshape(1, 1, slots, PAGE, 2, kv_width)


def solution(mesh):
    split = Mesh(mesh.devices.reshape(SIDE, SIDE, mesh.shape["section"], 2), ALL)
    in_specs = (
        P("section", "tensor", ROLL),
        P(None, "tensor", ROLL),
        P("section", ROLL, "tensor"),
        P("section", ROLL, None, "tensor"),
        P("section", "tensor", ROLL),
        P("section", "tensor"),
        P("section", None, "tensor"),
        P("section", ROLL),
        P(ROLL, "section", None, None, "tensor"),
        P(),
        P(),
        P(),
    )
    out_specs = (
        P("section", None, "tensor", ROLL),
        P(ROLL, "section", None, None, None, "tensor"),
    )
    return jax.shard_map(
        local, mesh=split, in_specs=in_specs, out_specs=out_specs, check_vma=False
    )
```

```python
import math

import jax
import jax.numpy as jnp
from jax import lax
from jax.experimental import pallas as pl
from jax.experimental.pallas import tpu as pltpu
from jax.sharding import Mesh, PartitionSpec as P

D = 8192
HD = 128
BLOCK = 32
BLOCKS = 3
PAGE = 32
SIDE = 4
SUMS = 128
ROLL = ("y", "x")
ALL = ("y", "x", "section", "tensor")
F32 = jnp.float32
BF16 = jnp.bfloat16


def dot(a, b):
    return jnp.dot(a, b, preferred_element_type=F32)


def params(megabytes):
    return pltpu.CompilerParams(vmem_limit_bytes=megabytes * 1024 * 1024)


def ring_routes(phase):
    routes = {}
    for shift in range(1, SIDE):
        route = []
        for y in range(SIDE):
            for x in range(SIDE):
                for s in range(SIDE):
                    for t in range(2):
                        along_x = t == phase
                        ty, tx = (y, (x + shift) % SIDE) if along_x else ((y + shift) % SIDE, x)
                        route.append(
                            (
                                ((y * SIDE + x) * SIDE + s) * 2 + t,
                                ((ty * SIDE + tx) * SIDE + s) * 2 + t,
                            )
                        )
        routes[shift] = route
    return routes


FIRST = ring_routes(0)
SECOND = ring_routes(1)


def ring(block, routes, shift):
    return lax.ppermute(block, ALL, routes[shift])


ORDER = (2, 1, 3, 0)
CHUNK = 1024


def fetch(wq_ref, wkv_ref, held, sems):
    copies = []
    for i in range(wq_ref.shape[1] // CHUNK):
        part = wq_ref.at[:, pl.ds(i * CHUNK, CHUNK)]
        copies.append(pltpu.make_async_copy(part, held.at[i], sems.at[i]))
    copies.append(pltpu.make_async_copy(wkv_ref, held.at[len(copies)], sems.at[len(copies)]))
    for copy in copies:
        copy.start()
    return copies


def lead_kernel(
    rows_ref, x_ref, far_ref, gain_ref, wq_ref, wkv_ref, o2a, o2b, scaled, squares, held, sems
):
    copies = fetch(wq_ref, wkv_ref, held, sems)
    half, depth = x_ref.shape
    count = 2 * half // (SIDE * SIDE)
    width = CHUNK * len(copies)
    gain = gain_ref[...].astype(F32)
    own = rows_ref[SIDE * SIDE]
    lead = []
    for n, first in enumerate(ORDER):
        for second in range(SIDE):
            at = rows_ref[first * SIDE + second] * count
            here = at // half == own
            at = pl.multiple_of(at % half, count)
            x = jnp.where(here, x_ref[pl.ds(at, count), :], far_ref[pl.ds(at, count), :])
            x = x.astype(F32)
            square = x * x
            sums = square[:, :SUMS]
            for low in range(SUMS, depth, SUMS):
                sums = sums + square[:, low : low + SUMS]
            value = (x * gain).astype(BF16)
            if n == 0:
                lead.append(value)
                out = (o2a, o2b)[second // 2]
                low = second % 2 * count
                out[low : low + count, width:] = sums.astype(BF16)
            else:
                low = ((n - 1) * SIDE + second) * count
                scaled[low : low + count, :] = value
                squares[low : low + count, :] = sums.astype(BF16)
    lead = jnp.concatenate(lead, axis=0)
    for i, copy in enumerate(copies):
        copy.wait()
        product = dot(lead, held[i]).astype(BF16)
        for n, out in enumerate((o2a, o2b)):
            out[:, i * CHUNK : (i + 1) * CHUNK] = product[n * 2 * count : (n + 1) * 2 * count]


def rest_kernel(scaled, squares, wq_ref, wkv_ref, *refs):
    outs = refs[:6]
    held, sems = refs[6:]
    copies = fetch(wq_ref, wkv_ref, held, sems)
    tokens = outs[0].shape[0]
    width = CHUNK * len(copies)
    value = scaled[...]
    for n, out in enumerate(outs):
        out[:, width:] = squares[n * tokens : (n + 1) * tokens, :]
    for i, copy in enumerate(copies):
        copy.wait()
        product = dot(value, held[i]).astype(BF16)
        for n, out in enumerate(outs):
            out[:, i * CHUNK : (i + 1) * CHUNK] = product[n * tokens : (n + 1) * tokens]


def project(rows, x, far, gain, wq, wkv):
    depth = x.shape[1]
    tokens = 2 * x.shape[0] // SIDE
    inner = wq.shape[1] + wkv.shape[1]
    chunks = inner // CHUNK
    vmem = pl.BlockSpec(memory_space=pltpu.VMEM)
    smem = pl.BlockSpec(memory_space=pltpu.SMEM)
    anywhere = pl.BlockSpec(memory_space=pl.ANY)
    block = jax.ShapeDtypeStruct((tokens // 2, inner + SUMS), BF16)
    scratch = [pltpu.VMEM((chunks, depth, CHUNK), BF16), pltpu.SemaphoreType.DMA((chunks,))]
    flops = 2 * tokens * depth * inner
    o2a, o2b, scaled, squares = pl.pallas_call(
        lead_kernel,
        in_specs=[smem, vmem, vmem, vmem, anywhere, anywhere],
        out_specs=[vmem] * 4,
        out_shape=[
            block,
            block,
            jax.ShapeDtypeStruct((3 * tokens, depth), BF16),
            jax.ShapeDtypeStruct((3 * tokens, SUMS), BF16),
        ],
        scratch_shapes=scratch,
        compiler_params=params(14),
        cost_estimate=pl.CostEstimate(
            flops=flops, bytes_accessed=6 * 2**20, transcendentals=0
        ),
        name="project_lead",
    )(rows, x, far, gain, wq, wkv)
    o1a, o1b, o3a, o3b, o0a, o0b = pl.pallas_call(
        rest_kernel,
        in_specs=[vmem, vmem, anywhere, anywhere],
        out_specs=[vmem] * 6,
        out_shape=[block] * 6,
        scratch_shapes=scratch,
        compiler_params=params(14),
        cost_estimate=pl.CostEstimate(
            flops=3 * flops, bytes_accessed=6 * 2**20, transcendentals=0
        ),
        name="project_rest",
    )(scaled, squares, wq, wkv)
    return (o0a, o0b), (o1a, o1b), (o2a, o2b), (o3a, o3b)


def add(*blocks):
    total = blocks[0].astype(F32)
    for block in blocks[1:]:
        total = total + block.astype(F32)
    return total.astype(BF16)


def first_sum(outs):
    (o0a, o0b), (o1a, o1b), (o2a, o2b), (o3a, o3b) = outs
    passing_a = ring(o2a, FIRST, 1)
    passing_b = ring(o2b, FIRST, SIDE - 1)
    from_behind_b = ring(o1b, FIRST, 1)
    from_ahead_a = ring(o3a, FIRST, SIDE - 1)
    from_behind_a = ring(add(o1a, passing_a), FIRST, 1)
    from_ahead_b = ring(add(o3b, passing_b), FIRST, SIDE - 1)
    return (o0a, from_ahead_a, from_behind_a), (o0b, from_behind_b, from_ahead_b)


def combine(halves):
    outs = []
    for blocks in halves:
        count = blocks[0].shape[0] // 2
        for low in (0, count):
            outs.append(add(*[block[low : low + count] for block in blocks]))
    return outs


def helpers(heads, parts, cos_ref, sin_ref, kvb_ref):
    kv_width = heads * HD
    query_width = 4 * kv_width

    def columns(low, high):
        total = parts[0][:, low:high].astype(F32)
        for part in parts[1:]:
            total = total + part[:, low:high].astype(F32)
        return total

    width = parts[0].shape[1]
    squares = jnp.sum(columns(width - SUMS, width), axis=1, keepdims=True)
    scale = lax.rsqrt(squares / D + 1e-06)
    cosine = cos_ref[...]
    sine = sin_ref[...]

    def rotate(values):
        return (values * cosine + pltpu.roll(values, HD // 2, 1) * sine).astype(BF16)

    def new_head(head):
        low = head * HD
        key = columns(query_width + low, query_width + low + HD) * scale
        key = rotate(key + kvb_ref[0:1, low : low + HD])
        low_value = query_width + kv_width + low
        val = columns(low_value, low_value + HD) * scale
        return key, (val + kvb_ref[1:2, low : low + HD]).astype(BF16)

    return columns, scale, rotate, new_head


def put_rows(rows, heads, head, key, val):
    count = key.shape[0]
    rows[pl.ds(2 * head, count, stride=2 * heads), :] = key.astype(F32)
    rows[pl.ds(2 * head + 1, count, stride=2 * heads), :] = val.astype(F32)


def attend_kernel(heads, past, *refs):
    (length_ref, p0, p1, p2, p3, cos_ref, sin_ref, qb_ref, kvb_ref, cache_ref) = refs[:10]
    if past:
        old_keys, old_vals = refs[10:12]
    out_ref, key_ref, val_ref, page_ref, held, sems, rows = refs[-7:]
    length = length_ref[0]
    copies = []
    for head in range(heads):
        for kind in range(2):
            part = cache_ref.at[:, pl.ds((kind * heads + head) * HD, HD)]
            at = 2 * head + kind
            copies.append(pltpu.make_async_copy(part, held.at[at], sems.at[at]))
            copies[-1].start()
    count = p0.shape[0]
    kv_width = heads * HD
    query_width = 4 * kv_width
    columns, scale, rotate, new_head = helpers(
        heads, (p0, p1, p2, p3), cos_ref, sin_ref, kvb_ref
    )

    context = cache_ref.shape[0]
    seen = lax.broadcasted_iota(jnp.int32, (1, context), 1) < length
    shape = (4 * count, past + count)
    token = lax.broadcasted_iota(jnp.int32, shape, 0) % count
    causal = lax.broadcasted_iota(jnp.int32, shape, 1) <= token + past
    factor = 1.0 / math.sqrt(HD)

    def scores(q, k):
        return lax.dot_general(q, k, (((1,), (1,)), ((), ())), preferred_element_type=F32)

    for head in range(heads):
        low = head * HD
        key, val = new_head(head)
        put_rows(rows, heads, head, key, val)
        key_ref[:, low : low + HD] = key
        val_ref[:, low : low + HD] = val
        if past:
            key = jnp.concatenate([old_keys[:, low : low + HD], key], axis=0)
            val = jnp.concatenate([old_vals[:, low : low + HD], val], axis=0)
        group = []
        for g in range(4):
            at = (head * 4 + g) * HD
            query = columns(at, at + HD) * scale + qb_ref[0:1, at : at + HD]
            group.append(rotate(query))
        query = jnp.concatenate(group, axis=0)
        copies[2 * head].wait()
        cached = jnp.where(seen, scores(query, held[2 * head]), -1e30)
        recent = jnp.where(causal, scores(query, key), -1e30)
        peak = jnp.maximum(
            jnp.max(cached, axis=1, keepdims=True), jnp.max(recent, axis=1, keepdims=True)
        )
        cached = jnp.exp((cached - peak) * factor)
        recent = jnp.exp((recent - peak) * factor)
        total = jnp.sum(cached, axis=1, keepdims=True) + jnp.sum(recent, axis=1, keepdims=True)
        copies[2 * head + 1].wait()
        mixed = dot(cached.astype(BF16), held[2 * head + 1]) + dot(recent.astype(BF16), val)
        mixed = (mixed / total).astype(BF16)
        for g in range(4):
            at = (head * 4 + g) * HD
            out_ref[:, at : at + HD] = mixed[g * count : (g + 1) * count]
    page_ref[...] = rows[...].astype(BF16)


def page_kernel(heads, p0, p1, p2, p3, cos_ref, sin_ref, kvb_ref, page_ref, rows):
    new_head = helpers(heads, (p0, p1, p2, p3), cos_ref, sin_ref, kvb_ref)[3]
    for head in range(heads):
        put_rows(rows, heads, head, *new_head(head))
    page_ref[...] = rows[...].astype(BF16)


def new_page(parts, cosine, sine, keyval_bias):
    heads = keyval_bias.shape[1] // HD
    page = (2 * heads * parts[0].shape[0], HD)
    vmem = pl.BlockSpec(memory_space=pltpu.VMEM)
    return pl.pallas_call(
        lambda *refs: page_kernel(heads, *refs),
        in_specs=[vmem] * 7,
        out_specs=vmem,
        out_shape=jax.ShapeDtypeStruct(page, BF16),
        scratch_shapes=[pltpu.VMEM(page, F32)],
        compiler_params=params(4),
        cost_estimate=pl.CostEstimate(flops=2**20, bytes_accessed=2**20, transcendentals=0),
        name="new_page",
    )(*parts, cosine, sine, keyval_bias)


def attend(length, parts, cosine, sine, query_bias, keyval_bias, cache, olds):
    kv_width = keyval_bias.shape[1]
    heads = kv_width // HD
    count = parts[0].shape[0]
    past = olds[0].shape[0] if olds else 0
    vmem = pl.BlockSpec(memory_space=pltpu.VMEM)
    smem = pl.BlockSpec(memory_space=pltpu.SMEM)
    anywhere = pl.BlockSpec(memory_space=pl.ANY)
    operands = [*parts, cosine, sine, query_bias, keyval_bias, cache, *olds]
    keys = cache.shape[0] + past + count
    return pl.pallas_call(
        lambda *refs: attend_kernel(heads, past, *refs),
        in_specs=[smem] + [vmem] * 8 + [anywhere] + [vmem] * len(olds),
        out_specs=[vmem] * 4,
        out_shape=[
            jax.ShapeDtypeStruct((count, 4 * kv_width), BF16),
            jax.ShapeDtypeStruct((count, kv_width), BF16),
            jax.ShapeDtypeStruct((count, kv_width), BF16),
            jax.ShapeDtypeStruct((2 * heads * count, HD), BF16),
        ],
        scratch_shapes=[
            pltpu.VMEM((2 * heads, cache.shape[0], HD), BF16),
            pltpu.SemaphoreType.DMA((2 * heads,)),
            pltpu.VMEM((2 * heads * count, HD), F32),
        ],
        compiler_params=params(16),
        cost_estimate=pl.CostEstimate(
            flops=16 * count * keys * kv_width,
            bytes_accessed=4 * 2**20,
            transcendentals=4 * count * heads * keys,
        ),
        name="attend",
    )(length, *operands)


def place_kernel(rows_ref, *refs):
    blocks = refs[:-2]
    mine_ref, other_ref = refs[-2:]
    half = mine_ref.shape[0]
    count = blocks[0].shape[0] // SIDE
    own = rows_ref[SIDE * SIDE] * half
    for first, block in enumerate(blocks):
        for second in range(SIDE):
            at = rows_ref[first * SIDE + second] * count - own
            here = (at >= 0) & (at < half)
            value = block[second * count : (second + 1) * count, :]

            @pl.when(here)
            def _():
                mine_ref[pl.ds(pl.multiple_of(at, count), count), :] = value

            @pl.when(jnp.logical_not(here))
            def _():
                there = jnp.where(at < 0, at + half, at - half)
                other_ref[pl.ds(pl.multiple_of(there, count), count), :] = value


def place(rows, blocks):
    tokens, width = blocks[0].shape
    vmem = pl.BlockSpec(memory_space=pltpu.VMEM)
    return pl.pallas_call(
        place_kernel,
        in_specs=[pl.BlockSpec(memory_space=pltpu.SMEM)] + [vmem] * len(blocks),
        out_specs=[vmem] * 2,
        out_shape=[jax.ShapeDtypeStruct((2 * tokens, width), BF16)] * 2,
        compiler_params=params(8),
        cost_estimate=pl.CostEstimate(flops=0, bytes_accessed=2**20, transcendentals=0),
        name="place",
    )(rows, *blocks)


def ship_kernel(table_ref, resident_ref, f0, f1, out_ref, held, arrival, sems):
    start = table_ref[table_ref.shape[0] - 1]
    whole = pltpu.make_async_copy(resident_ref, held, arrival)
    whole.start()
    whole.wait()

    def each(act):
        def body(p, carry):
            @pl.when(p < start)
            def _():
                act(held.at[p], p)

            return carry

        lax.fori_loop(0, held.shape[0], body, 0)
        act(f0, start)
        act(f1, start + 1)

    def copy(source, p):
        return pltpu.make_async_copy(source, out_ref.at[table_ref[p]], sems.at[p])

    each(lambda source, p: copy(source, p).start())
    each(lambda source, p: copy(source, p).wait())


def ship(table, resident, fresh, count):
    anywhere = pl.BlockSpec(memory_space=pl.ANY)
    vmem = pl.BlockSpec(memory_space=pltpu.VMEM)
    return pl.pallas_call(
        ship_kernel,
        in_specs=[pl.BlockSpec(memory_space=pltpu.SMEM), anywhere, vmem, vmem],
        out_specs=anywhere,
        out_shape=jax.ShapeDtypeStruct((count,) + resident.shape[1:], BF16),
        scratch_shapes=[
            pltpu.VMEM(resident.shape, BF16),
            pltpu.SemaphoreType.DMA,
            pltpu.SemaphoreType.DMA((table.shape[0] - 1,)),
        ],
        compiler_params=params(6),
        cost_estimate=pl.CostEstimate(flops=0, bytes_accessed=5 * 2**20, transcendentals=0),
        name="ship",
    )(table, resident, *fresh)


def ship_last_kernel(table_ref, page_ref, given_ref, out_ref, sem):
    at = table_ref[table_ref[table_ref.shape[0] - 1] + BLOCKS - 1]
    copy = pltpu.make_async_copy(page_ref, out_ref.at[at], sem)
    copy.start()
    copy.wait()


def ship_last(table, page, given):
    anywhere = pl.BlockSpec(memory_space=pl.ANY)
    vmem = pl.BlockSpec(memory_space=pltpu.VMEM)
    return pl.pallas_call(
        ship_last_kernel,
        in_specs=[pl.BlockSpec(memory_space=pltpu.SMEM), vmem, anywhere],
        out_specs=anywhere,
        out_shape=jax.ShapeDtypeStruct(given.shape, BF16),
        scratch_shapes=[pltpu.SemaphoreType.DMA],
        input_output_aliases={2: 0},
        compiler_params=params(4),
        cost_estimate=pl.CostEstimate(flops=0, bytes_accessed=2**18, transcendentals=0),
        name="ship_last",
    )(table, page, given)


def store_kernel(table_ref, arrived_ref, pool_ref, held, reads, writes):
    slots = pool_ref.shape[0]

    def read(q):
        source = jnp.maximum(table_ref[q], 0)
        return pltpu.make_async_copy(arrived_ref.at[source], held.at[q], reads.at[q])

    def write(q):
        return pltpu.make_async_copy(held.at[q], pool_ref.at[q], writes.at[q])

    def each(act):
        def body(q, carry):
            act(q)
            return carry

        lax.fori_loop(0, slots, body, 0)

    def begin(q):
        @pl.when(table_ref[q] >= 0)
        def _():
            read(q).start()

    def turn(q):
        @pl.when(table_ref[q] >= 0)
        def _():
            read(q).wait()

        @pl.when(table_ref[q] < 0)
        def _():
            held[q] = jnp.zeros(held.shape[1:], BF16)

        write(q).start()

    each(begin)
    each(turn)
    each(lambda q: write(q).wait())


def store(table, arrived, slots):
    anywhere = pl.BlockSpec(memory_space=pl.ANY)
    return pl.pallas_call(
        store_kernel,
        in_specs=[pl.BlockSpec(memory_space=pltpu.SMEM), anywhere],
        out_specs=anywhere,
        out_shape=jax.ShapeDtypeStruct((slots,) + arrived.shape[1:], BF16),
        scratch_shapes=[
            pltpu.VMEM((slots,) + arrived.shape[1:], BF16),
            pltpu.SemaphoreType.DMA((slots,)),
            pltpu.SemaphoreType.DMA((slots,)),
        ],
        compiler_params=params(60),
        cost_estimate=pl.CostEstimate(flops=0, bytes_accessed=5 * 2**20, transcendentals=0),
        name="store",
    )(table, arrived)


def local(
    entering,
    arriving,
    w_query,
    w_keyval,
    w_out,
    query_bias,
    keyval_bias,
    norm_gain,
    resident_kv,
    resumed_pages,
    section_active,
    block_table,
):
    section_count = lax.axis_size("section")
    y = lax.axis_index("y")
    x = lax.axis_index("x")
    section = lax.axis_index("section")
    tensor = lax.axis_index("tensor")
    rollout = y * SIDE + x
    roll_count = SIDE * SIDE
    kv_width = w_keyval.shape[3]
    wq = w_query[0]
    wkv = w_keyval[0].reshape(w_keyval.shape[1], 2 * kv_width)
    w_mix = w_out[0]
    length = resumed_pages[rollout] * PAGE + (section_count - 1 - section) * BLOCK
    active = section_active[section].astype(F32)

    first = jnp.arange(SIDE, dtype=jnp.int32)[:, None]
    second = jnp.arange(SIDE, dtype=jnp.int32)[None, :]
    by_x = ((second + y) % SIDE) * SIDE + (first + x) % SIDE
    by_y = ((first + y) % SIDE) * SIDE + (second + x) % SIDE
    rows = jnp.where(tensor == 0, by_x, by_y).reshape(-1)
    rows = jnp.concatenate([rows, tensor[None]]).astype(jnp.int32)

    half = HD // 2
    freq = jnp.power(F32(1000000.0), -(jnp.arange(half, dtype=F32) * (2.0 / HD)))
    positions = length + jnp.arange(BLOCKS * BLOCK, dtype=jnp.int32)
    angle = positions.astype(F32)[:, None] * freq[None, :]
    cosine = jnp.concatenate([jnp.cos(angle), jnp.cos(angle)], axis=1)
    sine = jnp.concatenate([-jnp.sin(angle), jnp.sin(angle)], axis=1)

    resident = resident_kv[0, 0]
    cache = resident.reshape(resident.shape[0], 2 * kv_width)
    query_shift = query_bias.astype(F32)
    keyval_shift = keyval_bias[0].astype(F32)
    swap = [(0, 1), (1, 0)]
    relay = [(i, i + 1) for i in range(section_count - 1)]

    dest_count = roll_count * section_count
    slots = block_table.shape[2]
    routing = block_table.reshape(dest_count, slots, 2)
    targets = routing[:, :, 0]
    slot_ids = routing[:, :, 1]
    own = rollout * section_count + section
    sources = jnp.arange(dest_count, dtype=jnp.int32)
    source_pages = (
        resumed_pages[:, None]
        + (section_count - 1 - jnp.arange(section_count, dtype=jnp.int32))[None, :]
        + BLOCKS
    )
    live_pages = jnp.where(section_active[None, :] > 0, source_pages, 0).reshape(-1)
    page_ids = jnp.arange(slots, dtype=jnp.int32)
    mine = (targets == own) & (page_ids[None, :] < live_pages[:, None])
    hit = mine[:, :, None] & (slot_ids[:, :, None] == page_ids)
    origin = jnp.max(jnp.where(hit, sources[:, None, None], -1), axis=(0, 1))
    sending = jnp.concatenate([targets[own], (length // PAGE)[None]]).astype(jnp.int32)

    heads = kv_width // HD
    pages = resident.reshape(-1, 2, heads, HD).swapaxes(1, 2).reshape(-1, PAGE * 2 * heads, HD)

    fresh_keys = []
    fresh_vals = []
    fresh = []
    results = []
    current = entering[0]
    for step in range(BLOCKS):
        last = step == BLOCKS - 1
        if step > 0:
            handed = lax.ppermute(results[-1], "section", relay)
            current = jnp.where(section == 0, arriving[step - 1], handed)
        far = lax.ppermute(current, "tensor", swap)
        outs = project(rows, current, far, norm_gain, wq, wkv)
        if last:
            slots_ahead, _ = lax.optimization_barrier((sending, outs))
            outgoing = ship(slots_ahead, pages, fresh, dest_count)
        outs = combine(first_sum(outs))
        if last:
            outs, outgoing = lax.optimization_barrier((outs, outgoing))
        parts = [outs[0]] + [ring(outs[d], SECOND, d) for d in (2, 1, 3)]
        at = slice(step * BLOCK, (step + 1) * BLOCK)
        if last:
            pass
        olds = []
        if fresh_keys:
            olds = [jnp.concatenate(fresh_keys), jnp.concatenate(fresh_vals)]
        attended, key, val, page = attend(
            length[None],
            parts,
            cosine[at],
            sine[at],
            query_shift,
            keyval_shift,
            cache,
            olds,
        )
        fresh_keys.append(key)
        fresh_vals.append(val)
        fresh.append(page)
        ahead, across, behind = [ring(attended, SECOND, SIDE - d) for d in range(1, SIDE)]
        gathered = jnp.concatenate([attended, ahead, across, behind])
        blocks = [gathered] + [ring(gathered, FIRST, SIDE - d) for d in range(1, SIDE)]
        if last:
            outgoing = ship_last(sending, page, outgoing)
            outgoing, _ = lax.optimization_barrier((outgoing, blocks[1:]))
            arrived = lax.all_to_all(outgoing, ROLL + ("section",), 0, 0, tiled=True)
        mine, other = place(rows, [dot(block, w_mix).astype(BF16) for block in blocks])
        theirs = lax.ppermute(other, "tensor", swap)
        summed = mine.astype(F32) + theirs.astype(F32)
        results.append((current.astype(F32) + active * summed).astype(BF16))
    section_out = jnp.stack(results)[None]

    pool = store(origin, arrived, slots)
    pool = pool.reshape(slots * PAGE, heads, 2, HD).swapaxes(1, 2)
    return section_out, pool.reshape(1, 1, slots, PAGE, 2, kv_width)


def solution(mesh):
    split = Mesh(mesh.devices.reshape(SIDE, SIDE, mesh.shape["section"], 2), ALL)
    in_specs = (
        P("section", "tensor", ROLL),
        P(None, "tensor", ROLL),
        P("section", ROLL, "tensor"),
        P("section", ROLL, None, "tensor"),
        P("section", "tensor", ROLL),
        P("section", "tensor"),
        P("section", None, "tensor"),
        P("section", ROLL),
        P(ROLL, "section", None, None, "tensor"),
        P(),
        P(),
        P(),
    )
    out_specs = (
        P("section", None, "tensor", ROLL),
        P(ROLL, "section", None, None, None, "tensor"),
    )
    return jax.shard_map(
        local, mesh=split, in_specs=in_specs, out_specs=out_specs, check_vma=False
    )
```

```python
import math

import jax
import jax.numpy as jnp
from jax import lax
from jax.experimental import pallas as pl
from jax.experimental.pallas import tpu as pltpu
from jax.sharding import Mesh, PartitionSpec as P

D = 8192
HD = 128
BLOCK = 32
BLOCKS = 3
PAGE = 32
SIDE = 4
SUMS = 128
ROLL = ("y", "x")
ALL = ("y", "x", "section", "tensor")
F32 = jnp.float32
BF16 = jnp.bfloat16


HBM = pl.BlockSpec(memory_space=pltpu.HBM)
VMEM = pl.BlockSpec(memory_space=pltpu.VMEM)
SMEM = pl.BlockSpec(memory_space=pltpu.SMEM)


def dot(a, b):
    return jnp.dot(a, b, preferred_element_type=F32)


def params(megabytes):
    return pltpu.CompilerParams(vmem_limit_bytes=megabytes * 1024 * 1024)


def ring_routes(phase):
    routes = {}
    for shift in range(1, SIDE):
        route = []
        for y in range(SIDE):
            for x in range(SIDE):
                for s in range(SIDE):
                    for t in range(2):
                        along_x = t == phase
                        ty, tx = (y, (x + shift) % SIDE) if along_x else ((y + shift) % SIDE, x)
                        route.append(
                            (
                                ((y * SIDE + x) * SIDE + s) * 2 + t,
                                ((ty * SIDE + tx) * SIDE + s) * 2 + t,
                            )
                        )
        routes[shift] = route
    return routes


FIRST = ring_routes(0)
SECOND = ring_routes(1)


def ring(block, routes, shift):
    return lax.ppermute(block, ALL, routes[shift])


def rollout_of(where, first, second):
    y, x = where[0], where[1]
    by_x = ((second + y) & 3) * SIDE + ((first + x) & 3)
    by_y = ((first + y) & 3) * SIDE + ((second + x) & 3)
    return jnp.where(where[3] == 0, by_x, by_y)


ORDER = (2, 1, 3, 0)
CHUNK = 1024


def fetch(wq_ref, wkv_ref, held, sems):
    copies = []
    for i in range(wq_ref.shape[1] // CHUNK):
        part = wq_ref.at[:, pl.ds(i * CHUNK, CHUNK)]
        copies.append(pltpu.make_async_copy(part, held.at[i], sems.at[i]))
    copies.append(pltpu.make_async_copy(wkv_ref, held.at[len(copies)], sems.at[len(copies)]))
    for copy in copies:
        copy.start()
    return copies


def lead_kernel(where, gain_ref, wq_ref, wkv_ref, *refs):
    x_ref, far_ref, *given = refs[:-6]
    o2a, o2b, scaled, squares, held, sems = refs[-6:]
    copies = fetch(wq_ref, wkv_ref, held, sems)
    half, depth = x_ref.shape
    count = 2 * half // (SIDE * SIDE)
    width = CHUNK * len(copies)
    gain = gain_ref[...].astype(F32)
    own = where[3]
    outside = where[2] == 0
    lead = []
    for n, first in enumerate(ORDER):
        for second in range(SIDE):
            at = rollout_of(where, first, second) * count
            here = at // half == own
            at = pl.multiple_of(at % half, count)
            x = jnp.where(here, x_ref[pl.ds(at, count), :], far_ref[pl.ds(at, count), :])
            if given:
                own_rows, far_rows = given[0][pl.ds(at, count), :], given[1][pl.ds(at, count), :]
                x = jnp.where(outside, jnp.where(here, own_rows, far_rows), x)
            x = x.astype(F32)
            square = x * x
            sums = square[:, :SUMS]
            for low in range(SUMS, depth, SUMS):
                sums = sums + square[:, low : low + SUMS]
            value = (x * gain).astype(BF16)
            if n == 0:
                lead.append(value)
                out = (o2a, o2b)[second // 2]
                low = second % 2 * count
                out[low : low + count, width:] = sums.astype(BF16)
            else:
                low = ((n - 1) * SIDE + second) * count
                scaled[low : low + count, :] = value
                squares[low : low + count, :] = sums.astype(BF16)
    lead = jnp.concatenate(lead, axis=0)
    for i, copy in enumerate(copies):
        copy.wait()
        product = dot(lead, held[i]).astype(BF16)
        for n, out in enumerate((o2a, o2b)):
            out[:, i * CHUNK : (i + 1) * CHUNK] = product[n * 2 * count : (n + 1) * 2 * count]


def rest_kernel(scaled, squares, wq_ref, wkv_ref, *refs):
    outs = refs[:6]
    held, sems = refs[6:]
    copies = fetch(wq_ref, wkv_ref, held, sems)
    tokens = outs[0].shape[0]
    width = CHUNK * len(copies)
    value = scaled[...]
    for n, out in enumerate(outs):
        out[:, width:] = squares[n * tokens : (n + 1) * tokens, :]
    for i, copy in enumerate(copies):
        copy.wait()
        product = dot(value, held[i]).astype(BF16)
        for n, out in enumerate(outs):
            out[:, i * CHUNK : (i + 1) * CHUNK] = product[n * tokens : (n + 1) * tokens]


def project(where, inputs, gain, wq, wkv):
    half, depth = inputs[0].shape
    tokens = 2 * half // SIDE
    inner = wq.shape[1] + wkv.shape[1]
    chunks = inner // CHUNK
    block = jax.ShapeDtypeStruct((tokens // 2, inner + SUMS), BF16)
    scratch = [pltpu.VMEM((chunks, depth, CHUNK), BF16), pltpu.SemaphoreType.DMA((chunks,))]
    flops = 2 * tokens * depth * inner
    o2a, o2b, scaled, squares = pl.pallas_call(
        lead_kernel,
        in_specs=[SMEM, VMEM, HBM, HBM] + [VMEM] * len(inputs),
        out_specs=[VMEM] * 4,
        out_shape=[
            block,
            block,
            jax.ShapeDtypeStruct((3 * tokens, depth), BF16),
            jax.ShapeDtypeStruct((3 * tokens, SUMS), BF16),
        ],
        scratch_shapes=scratch,
        compiler_params=params(14),
        cost_estimate=pl.CostEstimate(
            flops=flops, bytes_accessed=6 * 2**20, transcendentals=0
        ),
        name="project_lead",
    )(where, gain, wq, wkv, *inputs)
    o1a, o1b, o3a, o3b, o0a, o0b = pl.pallas_call(
        rest_kernel,
        in_specs=[VMEM, VMEM, HBM, HBM],
        out_specs=[VMEM] * 6,
        out_shape=[block] * 6,
        scratch_shapes=scratch,
        compiler_params=params(14),
        cost_estimate=pl.CostEstimate(
            flops=3 * flops, bytes_accessed=6 * 2**20, transcendentals=0
        ),
        name="project_rest",
    )(scaled, squares, wq, wkv)
    return (o0a, o0b), (o1a, o1b), (o2a, o2b), (o3a, o3b)


def add(*blocks):
    total = blocks[0].astype(F32)
    for block in blocks[1:]:
        total = total + block.astype(F32)
    return total.astype(BF16)


def first_sum(outs):
    (o0a, o0b), (o1a, o1b), (o2a, o2b), (o3a, o3b) = outs
    passing_a = ring(o2a, FIRST, 1)
    passing_b = ring(o2b, FIRST, SIDE - 1)
    from_behind_b = ring(o1b, FIRST, 1)
    from_ahead_a = ring(o3a, FIRST, SIDE - 1)
    from_behind_a = ring(add(o1a, passing_a), FIRST, 1)
    from_ahead_b = ring(add(o3b, passing_b), FIRST, SIDE - 1)
    return (o0a, from_ahead_a, from_behind_a), (o0b, from_behind_b, from_ahead_b)


def combine(halves):
    outs = []
    for blocks in halves:
        count = blocks[0].shape[0] // 2
        for low in (0, count):
            outs.append(add(*[block[low : low + count] for block in blocks]))
    return outs


def helpers(heads, parts, cos_ref, sin_ref, kvb_ref):
    kv_width = heads * HD
    query_width = 4 * kv_width

    def columns(low, high):
        total = parts[0][:, low:high].astype(F32)
        for part in parts[1:]:
            total = total + part[:, low:high].astype(F32)
        return total

    width = parts[0].shape[1]
    squares = jnp.sum(columns(width - SUMS, width), axis=1, keepdims=True)
    scale = lax.rsqrt(squares / D + 1e-06)
    cosine = cos_ref[...]
    sine = sin_ref[...]

    def rotate(values):
        return (values * cosine + pltpu.roll(values, HD // 2, 1) * sine).astype(BF16)

    def new_head(head):
        low = head * HD
        key = columns(query_width + low, query_width + low + HD) * scale
        key = rotate(key + kvb_ref[0:1, low : low + HD].astype(F32))
        low_value = query_width + kv_width + low
        val = columns(low_value, low_value + HD) * scale
        return key, (val + kvb_ref[1:2, low : low + HD].astype(F32)).astype(BF16)

    return columns, scale, rotate, new_head


def put_rows(rows, heads, head, key, val):
    count = key.shape[0]
    rows[pl.ds(2 * head, count, stride=2 * heads), :] = key.astype(F32)
    rows[pl.ds(2 * head + 1, count, stride=2 * heads), :] = val.astype(F32)


def attend_kernel(heads, past, *refs):
    (length_ref, p0, p1, p2, p3, cos_ref, sin_ref, qb_ref, kvb_ref, cache_ref) = refs[:10]
    if past:
        old_keys, old_vals = refs[10:12]
    out_ref, key_ref, val_ref, page_ref, held, sems, rows = refs[-7:]
    length = length_ref[0]
    copies = []
    for head in range(heads):
        for kind in range(2):
            part = cache_ref.at[:, pl.ds((kind * heads + head) * HD, HD)]
            at = 2 * head + kind
            copies.append(pltpu.make_async_copy(part, held.at[at], sems.at[at]))
            copies[-1].start()
    count = p0.shape[0]
    kv_width = heads * HD
    query_width = 4 * kv_width
    columns, scale, rotate, new_head = helpers(
        heads, (p0, p1, p2, p3), cos_ref, sin_ref, kvb_ref
    )

    context = cache_ref.shape[0]
    seen = lax.broadcasted_iota(jnp.int32, (1, context), 1) < length
    shape = (4 * count, past + count)
    token = lax.broadcasted_iota(jnp.int32, shape, 0) % count
    causal = lax.broadcasted_iota(jnp.int32, shape, 1) <= token + past
    factor = 1.0 / math.sqrt(HD)

    def scores(q, k):
        return lax.dot_general(q, k, (((1,), (1,)), ((), ())), preferred_element_type=F32)

    for head in range(heads):
        low = head * HD
        key, val = new_head(head)
        put_rows(rows, heads, head, key, val)
        key_ref[:, low : low + HD] = key
        val_ref[:, low : low + HD] = val
        if past:
            key = jnp.concatenate([old_keys[:, low : low + HD], key], axis=0)
            val = jnp.concatenate([old_vals[:, low : low + HD], val], axis=0)
        group = []
        for g in range(4):
            at = (head * 4 + g) * HD
            query = columns(at, at + HD) * scale + qb_ref[0:1, at : at + HD].astype(F32)
            group.append(rotate(query))
        query = jnp.concatenate(group, axis=0)
        copies[2 * head].wait()
        cached = jnp.where(seen, scores(query, held[2 * head]), -1e30)
        recent = jnp.where(causal, scores(query, key), -1e30)
        peak = jnp.maximum(
            jnp.max(cached, axis=1, keepdims=True), jnp.max(recent, axis=1, keepdims=True)
        )
        cached = jnp.exp((cached - peak) * factor)
        recent = jnp.exp((recent - peak) * factor)
        total = jnp.sum(cached, axis=1, keepdims=True) + jnp.sum(recent, axis=1, keepdims=True)
        copies[2 * head + 1].wait()
        mixed = dot(cached.astype(BF16), held[2 * head + 1]) + dot(recent.astype(BF16), val)
        mixed = (mixed / total).astype(BF16)
        for g in range(4):
            at = (head * 4 + g) * HD
            out_ref[:, at : at + HD] = mixed[g * count : (g + 1) * count]
    page_ref[...] = rows[...].astype(BF16)


def page_kernel(heads, p0, p1, p2, p3, cos_ref, sin_ref, kvb_ref, page_ref, rows):
    new_head = helpers(heads, (p0, p1, p2, p3), cos_ref, sin_ref, kvb_ref)[3]
    for head in range(heads):
        put_rows(rows, heads, head, *new_head(head))
    page_ref[...] = rows[...].astype(BF16)


def new_page(parts, cosine, sine, keyval_bias):
    heads = keyval_bias.shape[1] // HD
    page = (2 * heads * parts[0].shape[0], HD)
    return pl.pallas_call(
        lambda *refs: page_kernel(heads, *refs),
        in_specs=[VMEM] * 7,
        out_specs=VMEM,
        out_shape=jax.ShapeDtypeStruct(page, BF16),
        scratch_shapes=[pltpu.VMEM(page, F32)],
        compiler_params=params(4),
        cost_estimate=pl.CostEstimate(flops=2**20, bytes_accessed=2**20, transcendentals=0),
        name="new_page",
    )(*parts, cosine, sine, keyval_bias)


def attend(length, parts, cosine, sine, query_bias, keyval_bias, cache, olds):
    kv_width = keyval_bias.shape[1]
    heads = kv_width // HD
    count = parts[0].shape[0]
    past = olds[0].shape[0] if olds else 0
    operands = [*parts, cosine, sine, query_bias, keyval_bias, cache, *olds]
    keys = cache.shape[0] + past + count
    return pl.pallas_call(
        lambda *refs: attend_kernel(heads, past, *refs),
        in_specs=[SMEM] + [VMEM] * 8 + [HBM] + [VMEM] * len(olds),
        out_specs=[VMEM] * 4,
        out_shape=[
            jax.ShapeDtypeStruct((count, 4 * kv_width), BF16),
            jax.ShapeDtypeStruct((count, kv_width), BF16),
            jax.ShapeDtypeStruct((count, kv_width), BF16),
            jax.ShapeDtypeStruct((2 * heads * count, HD), BF16),
        ],
        scratch_shapes=[
            pltpu.VMEM((2 * heads, cache.shape[0], HD), BF16),
            pltpu.SemaphoreType.DMA((2 * heads,)),
            pltpu.VMEM((2 * heads * count, HD), F32),
        ],
        compiler_params=params(16),
        cost_estimate=pl.CostEstimate(
            flops=16 * count * keys * kv_width,
            bytes_accessed=4 * 2**20,
            transcendentals=4 * count * heads * keys,
        ),
        name="attend",
    )(length, *operands)


def join_kernel(*refs):
    out = refs[-1]
    count = refs[0].shape[0]
    for i, block in enumerate(refs[:-1]):
        out[i * count : (i + 1) * count, :] = block[...]


def join(blocks):
    count, width = blocks[0].shape
    return pl.pallas_call(
        join_kernel,
        in_specs=[VMEM] * len(blocks),
        out_specs=VMEM,
        out_shape=jax.ShapeDtypeStruct((len(blocks) * count, width), BF16),
        compiler_params=params(4),
        cost_estimate=pl.CostEstimate(flops=0, bytes_accessed=2**20, transcendentals=0),
        name="join",
    )(*blocks)


def place_kernel(where, *refs):
    blocks = refs[:-2]
    mine_ref, other_ref = refs[-2:]
    half = mine_ref.shape[0]
    count = blocks[0].shape[0] // SIDE
    own = where[3] * half
    for second, block in enumerate(blocks):
        for first in range(SIDE):
            at = rollout_of(where, first, second) * count - own
            here = (at >= 0) & (at < half)
            value = block[first * count : (first + 1) * count, :]

            @pl.when(here)
            def _():
                mine_ref[pl.ds(pl.multiple_of(at, count), count), :] = value

            @pl.when(jnp.logical_not(here))
            def _():
                there = jnp.where(at < 0, at + half, at - half)
                other_ref[pl.ds(pl.multiple_of(there, count), count), :] = value


def place(where, blocks):
    tokens, width = blocks[0].shape
    return pl.pallas_call(
        place_kernel,
        in_specs=[SMEM] + [VMEM] * len(blocks),
        out_specs=[VMEM] * 2,
        out_shape=[jax.ShapeDtypeStruct((2 * tokens, width), BF16)] * 2,
        compiler_params=params(8),
        cost_estimate=pl.CostEstimate(flops=0, bytes_accessed=2**20, transcendentals=0),
        name="place",
    )(where, *blocks)


def merge_kernel(stacked, where, active_ref, mine_ref, theirs_ref, x_ref, *refs):
    given, out_ref = refs[:-1], refs[-1]
    active = active_ref[where[2]].astype(F32)
    x = x_ref[...]
    if given:
        x = jnp.where(where[2] == 0, given[0][...], x)
    mixed = mine_ref[...].astype(F32) + theirs_ref[...].astype(F32)
    done = (x.astype(F32) + active * mixed).astype(BF16)
    if stacked:
        for i, before in enumerate(given[1:]):
            out_ref[i] = before[...]
        out_ref[len(given) - 1] = done
    else:
        out_ref[...] = done


def merge(where, active, mine, theirs, inputs, before=()):
    operands = [mine, theirs, *inputs, *before]
    shape = mine.shape
    if before:
        shape = (len(before) + 1,) + shape
    return pl.pallas_call(
        lambda *refs: merge_kernel(bool(before), *refs),
        in_specs=[SMEM, SMEM] + [VMEM] * len(operands),
        out_specs=VMEM,
        out_shape=jax.ShapeDtypeStruct(shape, BF16),
        compiler_params=params(8),
        cost_estimate=pl.CostEstimate(flops=2**20, bytes_accessed=2**20, transcendentals=0),
        name="merge",
    )(where, active, *operands)


def ship_kernel(table_ref, resident_ref, out_ref, held, arrival, sems):
    start = table_ref[table_ref.shape[0] - 1]
    whole = pltpu.make_async_copy(resident_ref, held, arrival)
    whole.start()
    whole.wait()

    def each(act):
        def body(p, carry):
            @pl.when(p < start)
            def _():
                act(held.at[p], p)

            return carry

        lax.fori_loop(0, held.shape[0], body, 0)

    def copy(source, p):
        return pltpu.make_async_copy(source, out_ref.at[table_ref[p]], sems.at[p])

    each(lambda source, p: copy(source, p).start())
    each(lambda source, p: copy(source, p).wait())


def ship(table, resident, count):
    return pl.pallas_call(
        ship_kernel,
        in_specs=[SMEM, HBM],
        out_specs=HBM,
        out_shape=jax.ShapeDtypeStruct((count,) + resident.shape[1:], BF16),
        scratch_shapes=[
            pltpu.VMEM(resident.shape, BF16),
            pltpu.SemaphoreType.DMA,
            pltpu.SemaphoreType.DMA((table.shape[0] - 1,)),
        ],
        compiler_params=params(61),
        cost_estimate=pl.CostEstimate(flops=0, bytes_accessed=5 * 2**20, transcendentals=0),
        name="ship",
    )(table, resident)


def ship_last_kernel(table_ref, f0, f1, f2, given_ref, out_ref, sems):
    start = table_ref[table_ref.shape[0] - 1]
    copies = [
        pltpu.make_async_copy(page, out_ref.at[table_ref[start + i]], sems.at[i])
        for i, page in enumerate((f0, f1, f2))
    ]
    for copy in copies:
        copy.start()
    for copy in copies:
        copy.wait()


def ship_last(table, fresh, given):
    return pl.pallas_call(
        ship_last_kernel,
        in_specs=[SMEM] + [VMEM] * BLOCKS + [HBM],
        out_specs=HBM,
        out_shape=jax.ShapeDtypeStruct(given.shape, BF16),
        scratch_shapes=[pltpu.SemaphoreType.DMA((BLOCKS,))],
        input_output_aliases={1 + BLOCKS: 0},
        compiler_params=params(61),
        cost_estimate=pl.CostEstimate(flops=0, bytes_accessed=2**18, transcendentals=0),
        name="ship_last",
    )(table, *fresh, given)


def store_kernel(table_ref, arrived_ref, pool_ref, held, reads, writes):
    slots = pool_ref.shape[0]

    def read(q):
        source = jnp.maximum(table_ref[q], 0)
        return pltpu.make_async_copy(arrived_ref.at[source], held.at[q], reads.at[q])

    def write(q):
        return pltpu.make_async_copy(held.at[q], pool_ref.at[q], writes.at[q])

    def each(act):
        def body(q, carry):
            act(q)
            return carry

        lax.fori_loop(0, slots, body, 0)

    def begin(q):
        @pl.when(table_ref[q] >= 0)
        def _():
            read(q).start()

    def turn(q):
        @pl.when(table_ref[q] >= 0)
        def _():
            read(q).wait()

        @pl.when(table_ref[q] < 0)
        def _():
            held[q] = jnp.zeros(held.shape[1:], BF16)

        write(q).start()

    each(begin)
    each(turn)
    each(lambda q: write(q).wait())


def store(table, arrived, slots):
    return pl.pallas_call(
        store_kernel,
        in_specs=[SMEM, HBM],
        out_specs=HBM,
        out_shape=jax.ShapeDtypeStruct((slots,) + arrived.shape[1:], BF16),
        scratch_shapes=[
            pltpu.VMEM((slots,) + arrived.shape[1:], BF16),
            pltpu.SemaphoreType.DMA((slots,)),
            pltpu.SemaphoreType.DMA((slots,)),
        ],
        compiler_params=params(6),
        cost_estimate=pl.CostEstimate(flops=0, bytes_accessed=5 * 2**20, transcendentals=0),
        name="store",
    )(table, arrived)


def local(
    entering,
    arriving,
    w_query,
    w_keyval,
    w_out,
    query_bias,
    keyval_bias,
    norm_gain,
    resident_kv,
    resumed_pages,
    section_active,
    block_table,
):
    section_count = lax.axis_size("section")
    y = lax.axis_index("y")
    x = lax.axis_index("x")
    section = lax.axis_index("section")
    tensor = lax.axis_index("tensor")
    rollout = y * SIDE + x
    roll_count = SIDE * SIDE
    kv_width = w_keyval.shape[3]
    wq = w_query[0]
    wkv = w_keyval[0].reshape(w_keyval.shape[1], 2 * kv_width)
    w_mix = w_out[0]
    length = resumed_pages[rollout] * PAGE + (section_count - 1 - section) * BLOCK

    where = jnp.stack([y, x, section, tensor]).astype(jnp.int32)

    half = HD // 2
    freq = jnp.power(F32(1000000.0), -(jnp.arange(half, dtype=F32) * (2.0 / HD)))
    positions = length + jnp.arange(BLOCKS * BLOCK, dtype=jnp.int32)
    angle = positions.astype(F32)[:, None] * freq[None, :]
    cosine = jnp.concatenate([jnp.cos(angle), jnp.cos(angle)], axis=1)
    sine = jnp.concatenate([-jnp.sin(angle), jnp.sin(angle)], axis=1)

    resident = resident_kv[0, 0]
    keyval_shift = keyval_bias[0]
    swap = [(0, 1), (1, 0)]
    relay = [(i, i + 1) for i in range(section_count - 1)]

    dest_count = roll_count * section_count
    slots = block_table.shape[2]
    routing = block_table.reshape(dest_count, slots, 2)
    targets = routing[:, :, 0]
    slot_ids = routing[:, :, 1]
    own = rollout * section_count + section
    sources = jnp.arange(dest_count, dtype=jnp.int32)
    source_pages = (
        resumed_pages[:, None]
        + (section_count - 1 - jnp.arange(section_count, dtype=jnp.int32))[None, :]
        + BLOCKS
    )
    live_pages = jnp.where(section_active[None, :] > 0, source_pages, 0).reshape(-1)
    page_ids = jnp.arange(slots, dtype=jnp.int32)
    mine = (targets == own) & (page_ids[None, :] < live_pages[:, None])
    hit = mine[:, :, None] & (slot_ids[:, :, None] == page_ids)
    origin = jnp.max(jnp.where(hit, sources[:, None, None], -1), axis=(0, 1))
    sending = jnp.concatenate([targets[own], (length // PAGE)[None]]).astype(jnp.int32)

    heads = kv_width // HD
    pages = resident.reshape(-1, 2, heads, HD).swapaxes(1, 2).reshape(-1, PAGE * 2 * heads, HD)

    fresh_keys = []
    fresh_vals = []
    fresh = []
    results = []
    arriving_far = lax.ppermute(arriving, "tensor", swap)
    for step in range(BLOCKS):
        last = step == BLOCKS - 1
        if step == 0:
            inputs = [entering[0], lax.ppermute(entering[0], "tensor", swap)]
        else:
            handed = lax.ppermute(results[-1], "section", relay)
            if step == 1:
                slots_ahead, _ = lax.optimization_barrier((sending, results[-1]))
                outgoing = ship(slots_ahead, pages, dest_count)
                handed, outgoing = lax.optimization_barrier((handed, outgoing))
            inputs = [handed, lax.ppermute(handed, "tensor", swap)]
            inputs += [arriving[step - 1], arriving_far[step - 1]]
        outs = project(where, inputs, norm_gain, wq, wkv)
        if step == 0:
            late, _ = lax.optimization_barrier((resident, outs))
            cache = late.reshape(resident.shape[0], 2 * kv_width)
        outs = combine(first_sum(outs))
        parts = [outs[0]] + [ring(outs[d], SECOND, d) for d in (2, 1, 3)]
        at = slice(step * BLOCK, (step + 1) * BLOCK)
        if last:
            fresh.append(new_page(parts, cosine[at], sine[at], keyval_shift))
            outgoing = ship_last(sending, fresh, outgoing)
            arrived = lax.all_to_all(outgoing, ROLL + ("section",), 0, 0, tiled=True)
            pool = store(origin, arrived, slots)
        olds = []
        if fresh_keys:
            olds = [jnp.concatenate(fresh_keys), jnp.concatenate(fresh_vals)]
        attended, key, val, page = attend(
            length[None],
            parts,
            cosine[at],
            sine[at],
            query_bias,
            keyval_shift,
            cache,
            olds,
        )
        fresh_keys.append(key)
        fresh_vals.append(val)
        fresh.append(page)
        ahead, across, behind = [ring(attended, FIRST, SIDE - d) for d in range(1, SIDE)]
        gathered = join([attended, ahead, across, behind])
        blocks = [gathered] + [ring(gathered, SECOND, SIDE - d) for d in range(1, SIDE)]
        if last:
            blocks[1], pool = lax.optimization_barrier((blocks[1], pool))
        mine, other = place(where, [dot(block, w_mix).astype(BF16) for block in blocks])
        theirs = lax.ppermute(other, "tensor", swap)
        kept = inputs[::2]
        results.append(merge(where, section_active, mine, theirs, kept, results if last else ()))
    section_out = results[-1][None]

    pool = pool.reshape(slots * PAGE, heads, 2, HD).swapaxes(1, 2)
    return section_out, pool.reshape(1, 1, slots, PAGE, 2, kv_width)


def solution(mesh):
    split = Mesh(mesh.devices.reshape(SIDE, SIDE, mesh.shape["section"], 2), ALL)
    in_specs = (
        P("section", "tensor", ROLL),
        P(None, "tensor", ROLL),
        P("section", ROLL, "tensor"),
        P("section", ROLL, None, "tensor"),
        P("section", "tensor", ROLL),
        P("section", "tensor"),
        P("section", None, "tensor"),
        P("section", ROLL),
        P(ROLL, "section", None, None, "tensor"),
        P(),
        P(),
        P(),
    )
    out_specs = (
        P("section", None, "tensor", ROLL),
        P(ROLL, "section", None, None, None, "tensor"),
    )
    return jax.shard_map(
        local, mesh=split, in_specs=in_specs, out_specs=out_specs, check_vma=False
    )
```

```python
import math

import jax
import jax.numpy as jnp
from jax import lax
from jax.experimental import pallas as pl
from jax.experimental.pallas import tpu as pltpu
from jax.sharding import Mesh, PartitionSpec as P

D = 8192
HD = 128
BLOCK = 32
BLOCKS = 3
PAGE = 32
SIDE = 4
SUMS = 128
ROLL = ("y", "x")
ALL = ("y", "x", "section", "tensor")
F32 = jnp.float32
BF16 = jnp.bfloat16


HBM = pl.BlockSpec(memory_space=pltpu.HBM)
VMEM = pl.BlockSpec(memory_space=pltpu.VMEM)
SMEM = pl.BlockSpec(memory_space=pltpu.SMEM)


def dot(a, b):
    return jnp.dot(a, b, preferred_element_type=F32)


def params(megabytes):
    return pltpu.CompilerParams(vmem_limit_bytes=megabytes * 1024 * 1024)


def ring_routes(phase):
    routes = {}
    for shift in range(1, SIDE):
        route = []
        for y in range(SIDE):
            for x in range(SIDE):
                for s in range(SIDE):
                    for t in range(2):
                        along_x = t == phase
                        ty, tx = (y, (x + shift) % SIDE) if along_x else ((y + shift) % SIDE, x)
                        route.append(
                            (
                                ((y * SIDE + x) * SIDE + s) * 2 + t,
                                ((ty * SIDE + tx) * SIDE + s) * 2 + t,
                            )
                        )
        routes[shift] = route
    return routes


FIRST = ring_routes(0)
SECOND = ring_routes(1)


def ring(block, routes, shift):
    return lax.ppermute(block, ALL, routes[shift])


def rollout_of(where, first, second):
    y, x = where[0], where[1]
    by_x = ((second + y) & 3) * SIDE + ((first + x) & 3)
    by_y = ((first + y) & 3) * SIDE + ((second + x) & 3)
    return jnp.where(where[3] == 0, by_x, by_y)


CHUNK = 1024


def fetch(wq_ref, wkv_ref, held, sems):
    copies = []
    for i in range(wq_ref.shape[1] // CHUNK):
        part = wq_ref.at[:, pl.ds(i * CHUNK, CHUNK)]
        copies.append(pltpu.make_async_copy(part, held.at[i], sems.at[i]))
    copies.append(pltpu.make_async_copy(wkv_ref, held.at[len(copies)], sems.at[len(copies)]))
    for copy in copies:
        copy.start()
    return copies


def project_kernel(firsts, where, gain_ref, wq_ref, wkv_ref, *refs):
    count_outs = 2 * len(firsts)
    x_ref, far_ref, *given = refs[: -count_outs - 3]
    outs = refs[-count_outs - 3 : -3]
    scaled, held, sems = refs[-3:]
    copies = fetch(wq_ref, wkv_ref, held, sems)
    half, depth = x_ref.shape
    count = 2 * half // (SIDE * SIDE)
    width = CHUNK * len(copies)
    gain = gain_ref[...].astype(F32)
    own = where[3]
    outside = where[2] == 0
    for n, first in enumerate(firsts):
        for second in range(SIDE):
            at = rollout_of(where, first, second) * count
            here = at // half == own
            at = pl.multiple_of(at % half, count)
            x = jnp.where(here, x_ref[pl.ds(at, count), :], far_ref[pl.ds(at, count), :])
            if given:
                own_rows, far_rows = given[0][pl.ds(at, count), :], given[1][pl.ds(at, count), :]
                x = jnp.where(outside, jnp.where(here, own_rows, far_rows), x)
            x = x.astype(F32)
            square = x * x
            sums = square[:, :SUMS]
            for low in range(SUMS, depth, SUMS):
                sums = sums + square[:, low : low + SUMS]
            low = (n * SIDE + second) * count
            scaled[low : low + count, :] = (x * gain).astype(BF16)
            low = second % 2 * count
            outs[2 * n + second // 2][low : low + count, width:] = sums.astype(BF16)
    value = scaled[...]
    for i, copy in enumerate(copies):
        copy.wait()
        product = dot(value, held[i]).astype(BF16)
        for n, out in enumerate(outs):
            low = n * 2 * count
            out[:, i * CHUNK : (i + 1) * CHUNK] = product[low : low + 2 * count]


def project(firsts, where, inputs, gain, wq, wkv):
    half, depth = inputs[0].shape
    tokens = 2 * half // SIDE
    inner = wq.shape[1] + wkv.shape[1]
    chunks = inner // CHUNK
    block = jax.ShapeDtypeStruct((tokens // 2, inner + SUMS), BF16)
    outs = pl.pallas_call(
        lambda *refs: project_kernel(firsts, *refs),
        in_specs=[SMEM, VMEM, HBM, HBM] + [VMEM] * len(inputs),
        out_specs=[VMEM] * (2 * len(firsts)),
        out_shape=[block] * (2 * len(firsts)),
        scratch_shapes=[
            pltpu.VMEM((len(firsts) * tokens, depth), BF16),
            pltpu.VMEM((chunks, depth, CHUNK), BF16),
            pltpu.SemaphoreType.DMA((chunks,)),
        ],
        compiler_params=params(10),
        cost_estimate=pl.CostEstimate(
            flops=2 * len(firsts) * tokens * depth * inner,
            bytes_accessed=6 * 2**20,
            transcendentals=0,
        ),
        name="project_lead" if len(firsts) == 1 else "project_rest",
    )(where, gain, wq, wkv, *inputs)
    return {first: tuple(outs[2 * n : 2 * n + 2]) for n, first in enumerate(firsts)}


def add(*blocks):
    total = blocks[0].astype(F32)
    for block in blocks[1:]:
        total = total + block.astype(F32)
    return total.astype(BF16)


def first_sum(outs):
    (o0a, o0b), (o1a, o1b), (o2a, o2b), (o3a, o3b) = [outs[d] for d in range(SIDE)]
    passing_a = ring(o2a, FIRST, 1)
    passing_b = ring(o2b, FIRST, SIDE - 1)
    from_behind_b = ring(o1b, FIRST, 1)
    from_ahead_a = ring(o3a, FIRST, SIDE - 1)
    from_behind_a = ring(add(o1a, passing_a), FIRST, 1)
    from_ahead_b = ring(add(o3b, passing_b), FIRST, SIDE - 1)
    return (o0a, from_ahead_a, from_behind_a), (o0b, from_behind_b, from_ahead_b)


def combine(halves):
    outs = []
    for blocks in halves:
        count = blocks[0].shape[0] // 2
        for low in (0, count):
            outs.append(add(*[block[low : low + count] for block in blocks]))
    return outs


def helpers(heads, parts, cos_ref, sin_ref, kvb_ref):
    kv_width = heads * HD
    query_width = 4 * kv_width

    def columns(low, high):
        total = parts[0][:, low:high].astype(F32)
        for part in parts[1:]:
            total = total + part[:, low:high].astype(F32)
        return total

    width = parts[0].shape[1]
    squares = jnp.sum(columns(width - SUMS, width), axis=1, keepdims=True)
    scale = lax.rsqrt(squares / D + 1e-06)
    cosine = cos_ref[...]
    sine = sin_ref[...]

    def rotate(values):
        return (values * cosine + pltpu.roll(values, HD // 2, 1) * sine).astype(BF16)

    def new_head(head):
        low = head * HD
        key = columns(query_width + low, query_width + low + HD) * scale
        key = rotate(key + kvb_ref[0:1, low : low + HD].astype(F32))
        low_value = query_width + kv_width + low
        val = columns(low_value, low_value + HD) * scale
        return key, (val + kvb_ref[1:2, low : low + HD].astype(F32)).astype(BF16)

    return columns, scale, rotate, new_head


def put_rows(rows, heads, head, key, val):
    count = key.shape[0]
    rows[pl.ds(2 * head, count, stride=2 * heads), :] = key.astype(F32)
    rows[pl.ds(2 * head + 1, count, stride=2 * heads), :] = val.astype(F32)


def attend_kernel(heads, past, *refs):
    (length_ref, p0, p1, p2, p3, cos_ref, sin_ref, qb_ref, kvb_ref, cache_ref) = refs[:10]
    if past:
        old_keys, old_vals = refs[10:12]
    out_ref, key_ref, val_ref, page_ref, held, sems, rows = refs[-7:]
    length = length_ref[0]
    copies = []
    for head in range(heads):
        for kind in range(2):
            part = cache_ref.at[:, pl.ds((kind * heads + head) * HD, HD)]
            at = 2 * head + kind
            copies.append(pltpu.make_async_copy(part, held.at[at], sems.at[at]))
            copies[-1].start()
    count = p0.shape[0]
    kv_width = heads * HD
    query_width = 4 * kv_width
    columns, scale, rotate, new_head = helpers(
        heads, (p0, p1, p2, p3), cos_ref, sin_ref, kvb_ref
    )

    context = cache_ref.shape[0]
    seen = lax.broadcasted_iota(jnp.int32, (1, context), 1) < length
    shape = (4 * count, past + count)
    token = lax.broadcasted_iota(jnp.int32, shape, 0) % count
    causal = lax.broadcasted_iota(jnp.int32, shape, 1) <= token + past
    factor = 1.0 / math.sqrt(HD)

    def scores(q, k):
        return lax.dot_general(q, k, (((1,), (1,)), ((), ())), preferred_element_type=F32)

    for head in range(heads):
        low = head * HD
        key, val = new_head(head)
        put_rows(rows, heads, head, key, val)
        key_ref[:, low : low + HD] = key
        val_ref[:, low : low + HD] = val
        if past:
            key = jnp.concatenate([old_keys[:, low : low + HD], key], axis=0)
            val = jnp.concatenate([old_vals[:, low : low + HD], val], axis=0)
        group = []
        for g in range(4):
            at = (head * 4 + g) * HD
            query = columns(at, at + HD) * scale + qb_ref[0:1, at : at + HD].astype(F32)
            group.append(rotate(query))
        query = jnp.concatenate(group, axis=0)
        copies[2 * head].wait()
        cached = jnp.where(seen, scores(query, held[2 * head]), -1e30)
        recent = jnp.where(causal, scores(query, key), -1e30)
        peak = jnp.maximum(
            jnp.max(cached, axis=1, keepdims=True), jnp.max(recent, axis=1, keepdims=True)
        )
        cached = jnp.exp((cached - peak) * factor)
        recent = jnp.exp((recent - peak) * factor)
        total = jnp.sum(cached, axis=1, keepdims=True) + jnp.sum(recent, axis=1, keepdims=True)
        copies[2 * head + 1].wait()
        mixed = dot(cached.astype(BF16), held[2 * head + 1]) + dot(recent.astype(BF16), val)
        mixed = (mixed / total).astype(BF16)
        for g in range(4):
            at = (head * 4 + g) * HD
            out_ref[:, at : at + HD] = mixed[g * count : (g + 1) * count]
    page_ref[...] = rows[...].astype(BF16)


def page_kernel(heads, p0, p1, p2, p3, cos_ref, sin_ref, kvb_ref, page_ref, rows):
    new_head = helpers(heads, (p0, p1, p2, p3), cos_ref, sin_ref, kvb_ref)[3]
    for head in range(heads):
        put_rows(rows, heads, head, *new_head(head))
    page_ref[...] = rows[...].astype(BF16)


def new_page(parts, cosine, sine, keyval_bias):
    heads = keyval_bias.shape[1] // HD
    page = (2 * heads * parts[0].shape[0], HD)
    return pl.pallas_call(
        lambda *refs: page_kernel(heads, *refs),
        in_specs=[VMEM] * 7,
        out_specs=VMEM,
        out_shape=jax.ShapeDtypeStruct(page, BF16),
        scratch_shapes=[pltpu.VMEM(page, F32)],
        compiler_params=params(4),
        cost_estimate=pl.CostEstimate(flops=2**20, bytes_accessed=2**20, transcendentals=0),
        name="new_page",
    )(*parts, cosine, sine, keyval_bias)


def attend(length, parts, cosine, sine, query_bias, keyval_bias, cache, olds):
    kv_width = keyval_bias.shape[1]
    heads = kv_width // HD
    count = parts[0].shape[0]
    past = olds[0].shape[0] if olds else 0
    operands = [*parts, cosine, sine, query_bias, keyval_bias, cache, *olds]
    keys = cache.shape[0] + past + count
    return pl.pallas_call(
        lambda *refs: attend_kernel(heads, past, *refs),
        in_specs=[SMEM] + [VMEM] * 8 + [HBM] + [VMEM] * len(olds),
        out_specs=[VMEM] * 4,
        out_shape=[
            jax.ShapeDtypeStruct((count, 4 * kv_width), BF16),
            jax.ShapeDtypeStruct((count, kv_width), BF16),
            jax.ShapeDtypeStruct((count, kv_width), BF16),
            jax.ShapeDtypeStruct((2 * heads * count, HD), BF16),
        ],
        scratch_shapes=[
            pltpu.VMEM((2 * heads, cache.shape[0], HD), BF16),
            pltpu.SemaphoreType.DMA((2 * heads,)),
            pltpu.VMEM((2 * heads * count, HD), F32),
        ],
        compiler_params=params(8),
        cost_estimate=pl.CostEstimate(
            flops=16 * count * keys * kv_width,
            bytes_accessed=4 * 2**20,
            transcendentals=4 * count * heads * keys,
        ),
        name="attend",
    )(length, *operands)


def join_kernel(*refs):
    out = refs[-1]
    count = refs[0].shape[0]
    for i, block in enumerate(refs[:-1]):
        out[i * count : (i + 1) * count, :] = block[...]


def join(blocks):
    count, width = blocks[0].shape
    return pl.pallas_call(
        join_kernel,
        in_specs=[VMEM] * len(blocks),
        out_specs=VMEM,
        out_shape=jax.ShapeDtypeStruct((len(blocks) * count, width), BF16),
        compiler_params=params(4),
        cost_estimate=pl.CostEstimate(flops=0, bytes_accessed=2**20, transcendentals=0),
        name="join",
    )(*blocks)


def gate_kernel(block_ref, ready_ref, out_ref):
    del block_ref, ready_ref, out_ref


def gate(block, ready):
    anywhere = pl.BlockSpec(memory_space=pl.ANY)
    return pl.pallas_call(
        gate_kernel,
        in_specs=[anywhere, anywhere],
        out_specs=anywhere,
        out_shape=jax.ShapeDtypeStruct(block.shape, block.dtype),
        input_output_aliases={0: 0},
        compiler_params=params(4),
        name="gate",
    )(block, ready)


def place_kernel(where, *refs):
    blocks = refs[:-2]
    mine_ref, other_ref = refs[-2:]
    half = mine_ref.shape[0]
    count = blocks[0].shape[0] // SIDE
    own = where[3] * half
    for second, block in enumerate(blocks):
        for first in range(SIDE):
            at = rollout_of(where, first, second) * count - own
            here = (at >= 0) & (at < half)
            value = block[first * count : (first + 1) * count, :]

            @pl.when(here)
            def _():
                mine_ref[pl.ds(pl.multiple_of(at, count), count), :] = value

            @pl.when(jnp.logical_not(here))
            def _():
                there = jnp.where(at < 0, at + half, at - half)
                other_ref[pl.ds(pl.multiple_of(there, count), count), :] = value


def place(where, blocks):
    tokens, width = blocks[0].shape
    return pl.pallas_call(
        place_kernel,
        in_specs=[SMEM] + [VMEM] * len(blocks),
        out_specs=[VMEM] * 2,
        out_shape=[jax.ShapeDtypeStruct((2 * tokens, width), BF16)] * 2,
        compiler_params=params(8),
        cost_estimate=pl.CostEstimate(flops=0, bytes_accessed=2**20, transcendentals=0),
        name="place",
    )(where, *blocks)


def merge_kernel(stacked, where, active_ref, mine_ref, theirs_ref, x_ref, *refs):
    given, out_ref = refs[:-1], refs[-1]
    active = active_ref[where[2]].astype(F32)
    x = x_ref[...]
    if given:
        x = jnp.where(where[2] == 0, given[0][...], x)
    mixed = mine_ref[...].astype(F32) + theirs_ref[...].astype(F32)
    done = (x.astype(F32) + active * mixed).astype(BF16)
    if stacked:
        for i, before in enumerate(given[1:]):
            out_ref[i] = before[...]
        out_ref[len(given) - 1] = done
    else:
        out_ref[...] = done


def merge(where, active, mine, theirs, inputs, before=()):
    operands = [mine, theirs, *inputs, *before]
    shape = mine.shape
    if before:
        shape = (len(before) + 1,) + shape
    return pl.pallas_call(
        lambda *refs: merge_kernel(bool(before), *refs),
        in_specs=[SMEM, SMEM] + [VMEM] * len(operands),
        out_specs=VMEM,
        out_shape=jax.ShapeDtypeStruct(shape, BF16),
        compiler_params=params(8),
        cost_estimate=pl.CostEstimate(flops=2**20, bytes_accessed=2**20, transcendentals=0),
        name="merge",
    )(where, active, *operands)


def ship_kernel(table_ref, resident_ref, out_ref, held, arrival, sems):
    start = table_ref[table_ref.shape[0] - 1]
    whole = pltpu.make_async_copy(resident_ref, held, arrival)
    whole.start()
    whole.wait()

    def each(act):
        def body(p, carry):
            @pl.when(p < start)
            def _():
                act(held.at[p], p)

            return carry

        lax.fori_loop(0, held.shape[0], body, 0)

    def copy(source, p):
        return pltpu.make_async_copy(source, out_ref.at[table_ref[p]], sems.at[p])

    each(lambda source, p: copy(source, p).start())
    each(lambda source, p: copy(source, p).wait())


def ship(table, resident, count):
    return pl.pallas_call(
        ship_kernel,
        in_specs=[SMEM, HBM],
        out_specs=HBM,
        out_shape=jax.ShapeDtypeStruct((count,) + resident.shape[1:], BF16),
        scratch_shapes=[
            pltpu.VMEM(resident.shape, BF16),
            pltpu.SemaphoreType.DMA,
            pltpu.SemaphoreType.DMA((table.shape[0] - 1,)),
        ],
        compiler_params=params(40),
        cost_estimate=pl.CostEstimate(flops=0, bytes_accessed=5 * 2**20, transcendentals=0),
        name="ship",
    )(table, resident)


def ship_last_kernel(table_ref, f0, f1, f2, given_ref, out_ref, sems):
    start = table_ref[table_ref.shape[0] - 1]
    copies = [
        pltpu.make_async_copy(page, out_ref.at[table_ref[start + i]], sems.at[i])
        for i, page in enumerate((f0, f1, f2))
    ]
    for copy in copies:
        copy.start()
    for copy in copies:
        copy.wait()


def ship_last(table, fresh, given):
    return pl.pallas_call(
        ship_last_kernel,
        in_specs=[SMEM] + [VMEM] * BLOCKS + [HBM],
        out_specs=HBM,
        out_shape=jax.ShapeDtypeStruct(given.shape, BF16),
        scratch_shapes=[pltpu.SemaphoreType.DMA((BLOCKS,))],
        input_output_aliases={1 + BLOCKS: 0},
        compiler_params=params(40),
        cost_estimate=pl.CostEstimate(flops=0, bytes_accessed=2**18, transcendentals=0),
        name="ship_last",
    )(table, *fresh, given)


def store_kernel(table_ref, arrived_ref, pool_ref, held, reads, writes):
    slots = pool_ref.shape[0]

    def read(q):
        source = jnp.maximum(table_ref[q], 0)
        return pltpu.make_async_copy(arrived_ref.at[source], held.at[q], reads.at[q])

    def write(q):
        return pltpu.make_async_copy(held.at[q], pool_ref.at[q], writes.at[q])

    def each(act):
        def body(q, carry):
            act(q)
            return carry

        lax.fori_loop(0, slots, body, 0)

    def begin(q):
        @pl.when(table_ref[q] >= 0)
        def _():
            read(q).start()

    def turn(q):
        @pl.when(table_ref[q] >= 0)
        def _():
            read(q).wait()

        @pl.when(table_ref[q] < 0)
        def _():
            held[q] = jnp.zeros(held.shape[1:], BF16)

        write(q).start()

    each(begin)
    each(turn)
    each(lambda q: write(q).wait())


def store(table, arrived, slots):
    return pl.pallas_call(
        store_kernel,
        in_specs=[SMEM, HBM],
        out_specs=HBM,
        out_shape=jax.ShapeDtypeStruct((slots,) + arrived.shape[1:], BF16),
        scratch_shapes=[
            pltpu.VMEM((slots,) + arrived.shape[1:], BF16),
            pltpu.SemaphoreType.DMA((slots,)),
            pltpu.SemaphoreType.DMA((slots,)),
        ],
        compiler_params=params(6),
        cost_estimate=pl.CostEstimate(flops=0, bytes_accessed=5 * 2**20, transcendentals=0),
        name="store",
    )(table, arrived)


def local(
    entering,
    arriving,
    w_query,
    w_keyval,
    w_out,
    query_bias,
    keyval_bias,
    norm_gain,
    resident_kv,
    resumed_pages,
    section_active,
    block_table,
):
    section_count = lax.axis_size("section")
    y = lax.axis_index("y")
    x = lax.axis_index("x")
    section = lax.axis_index("section")
    tensor = lax.axis_index("tensor")
    rollout = y * SIDE + x
    roll_count = SIDE * SIDE
    kv_width = w_keyval.shape[3]
    wq = w_query[0]
    wkv = w_keyval[0].reshape(w_keyval.shape[1], 2 * kv_width)
    w_mix = w_out[0]
    length = resumed_pages[rollout] * PAGE + (section_count - 1 - section) * BLOCK

    where = jnp.stack([y, x, section, tensor]).astype(jnp.int32)

    half = HD // 2
    freq = jnp.power(F32(1000000.0), -(jnp.arange(half, dtype=F32) * (2.0 / HD)))
    positions = length + jnp.arange(BLOCKS * BLOCK, dtype=jnp.int32)
    angle = positions.astype(F32)[:, None] * freq[None, :]
    cosine = jnp.concatenate([jnp.cos(angle), jnp.cos(angle)], axis=1)
    sine = jnp.concatenate([-jnp.sin(angle), jnp.sin(angle)], axis=1)

    resident = resident_kv[0, 0]
    keyval_shift = keyval_bias[0]
    swap = [(0, 1), (1, 0)]
    relay = [(i, i + 1) for i in range(section_count - 1)]

    dest_count = roll_count * section_count
    slots = block_table.shape[2]
    routing = block_table.reshape(dest_count, slots, 2)
    targets = routing[:, :, 0]
    slot_ids = routing[:, :, 1]
    own = rollout * section_count + section
    sources = jnp.arange(dest_count, dtype=jnp.int32)
    source_pages = (
        resumed_pages[:, None]
        + (section_count - 1 - jnp.arange(section_count, dtype=jnp.int32))[None, :]
        + BLOCKS
    )
    live_pages = jnp.where(section_active[None, :] > 0, source_pages, 0).reshape(-1)
    page_ids = jnp.arange(slots, dtype=jnp.int32)
    mine = (targets == own) & (page_ids[None, :] < live_pages[:, None])
    hit = mine[:, :, None] & (slot_ids[:, :, None] == page_ids)
    origin = jnp.max(jnp.where(hit, sources[:, None, None], -1), axis=(0, 1))

    def table_of(block_table):
        slots_of = block_table.reshape(dest_count, slots, 2)[own, :, 0]
        return jnp.concatenate([slots_of, (length // PAGE)[None]]).astype(jnp.int32)


    heads = kv_width // HD
    pages = resident.reshape(-1, 2, heads, HD).swapaxes(1, 2).reshape(-1, PAGE * 2 * heads, HD)

    fresh_keys = []
    fresh_vals = []
    fresh = []
    results = []
    for step in range(BLOCKS):
        last = step == BLOCKS - 1
        if step == 0:
            inputs = [entering[0], lax.ppermute(entering[0], "tensor", swap)]
        else:
            handed = lax.ppermute(results[-1], "section", relay)
            if step == 1:
                slots_ahead, _ = lax.optimization_barrier((early[-1], results[-1]))
                outgoing = ship(slots_ahead, pages, dest_count)
                handed, outgoing = lax.optimization_barrier((handed, outgoing))
            inputs = [handed, lax.ppermute(handed, "tensor", swap)]
            inputs += early[2 * step - 2 : 2 * step]
        outs = project((2,), where, inputs, norm_gain, wq, wkv)
        outs.update(project((1, 3, 0), where, inputs, norm_gain, wq, wkv))
        if step == 0:
            late, given, table, outs[0] = lax.optimization_barrier(
                (resident, arriving, block_table, outs[0])
            )
            table = table_of(table)
            cache = late.reshape(resident.shape[0], 2 * kv_width)
            given_far = lax.ppermute(given, "tensor", swap)
            early = [given[0], given_far[0], given[1], given_far[1], table]
        outs = combine(first_sum(outs))
        if step == 0:
            outs, early = lax.optimization_barrier((outs, early))
        parts = [outs[0]] + [ring(outs[d], SECOND, d) for d in (2, 1, 3)]
        at = slice(step * BLOCK, (step + 1) * BLOCK)
        if last:
            fresh.append(new_page(parts, cosine[at], sine[at], keyval_shift))
            outgoing = ship_last(early[-1], fresh, outgoing)
            arrived = lax.all_to_all(outgoing, ROLL + ("section",), 0, 0, tiled=True)
            pool = store(origin, arrived, slots)
        olds = []
        if fresh_keys:
            olds = [jnp.concatenate(fresh_keys), jnp.concatenate(fresh_vals)]
        attended, key, val, page = attend(
            length[None],
            parts,
            cosine[at],
            sine[at],
            query_bias,
            keyval_shift,
            cache,
            olds,
        )
        fresh_keys.append(key)
        fresh_vals.append(val)
        fresh.append(page)
        ahead, across, behind = [ring(attended, FIRST, SIDE - d) for d in range(1, SIDE)]
        gathered = join([attended, ahead, across, behind])
        if not last:
            gathered = gate(gathered, lax.ppermute(gathered[:16, :HD], "tensor", swap))
        blocks = [gathered] + [ring(gathered, SECOND, SIDE - d) for d in range(1, SIDE)]
        if last:
            blocks[1], pool = lax.optimization_barrier((blocks[1], pool))
        mine, other = place(where, [dot(block, w_mix).astype(BF16) for block in blocks])
        theirs = lax.ppermute(other, "tensor", swap)
        kept = inputs[::2]
        results.append(merge(where, section_active, mine, theirs, kept, results if last else ()))
    section_out = results[-1][None]

    pool = pool.reshape(slots * PAGE, heads, 2, HD).swapaxes(1, 2)
    return section_out, pool.reshape(1, 1, slots, PAGE, 2, kv_width)


def solution(mesh):
    split = Mesh(mesh.devices.reshape(SIDE, SIDE, mesh.shape["section"], 2), ALL)
    in_specs = (
        P("section", "tensor", ROLL),
        P(None, "tensor", ROLL),
        P("section", ROLL, "tensor"),
        P("section", ROLL, None, "tensor"),
        P("section", "tensor", ROLL),
        P("section", "tensor"),
        P("section", None, "tensor"),
        P("section", ROLL),
        P(ROLL, "section", None, None, "tensor"),
        P(),
        P(),
        P(),
    )
    out_specs = (
        P("section", None, "tensor", ROLL),
        P(ROLL, "section", None, None, None, "tensor"),
    )
    return jax.shard_map(
        local, mesh=split, in_specs=in_specs, out_specs=out_specs, check_vma=False
    )
```

```python
import math

import jax
import jax.numpy as jnp
from jax import lax
from jax.experimental import pallas as pl
from jax.experimental.pallas import tpu as pltpu
from jax.sharding import Mesh, PartitionSpec as P

D = 8192
HD = 128
BLOCK = 32
BLOCKS = 3
PAGE = 32
SIDE = 4
SUMS = 128
ROLL = ("y", "x")
ALL = ("y", "x", "section", "tensor")
F32 = jnp.float32
BF16 = jnp.bfloat16


HBM = pl.BlockSpec(memory_space=pltpu.HBM)
VMEM = pl.BlockSpec(memory_space=pltpu.VMEM)
SMEM = pl.BlockSpec(memory_space=pltpu.SMEM)


def dot(a, b):
    return jnp.dot(a, b, preferred_element_type=F32)


def params(megabytes):
    return pltpu.CompilerParams(vmem_limit_bytes=megabytes * 1024 * 1024)


def ring_routes(phase):
    routes = {}
    for shift in range(1, SIDE):
        route = []
        for y in range(SIDE):
            for x in range(SIDE):
                for s in range(SIDE):
                    for t in range(2):
                        along_x = t == phase
                        ty, tx = (y, (x + shift) % SIDE) if along_x else ((y + shift) % SIDE, x)
                        route.append(
                            (
                                ((y * SIDE + x) * SIDE + s) * 2 + t,
                                ((ty * SIDE + tx) * SIDE + s) * 2 + t,
                            )
                        )
        routes[shift] = route
    return routes


FIRST = ring_routes(0)
SECOND = ring_routes(1)


def ring(block, routes, shift):
    return lax.ppermute(block, ALL, routes[shift])


def rollout_of(where, first, second):
    y, x = where[0], where[1]
    by_x = ((second + y) & 3) * SIDE + ((first + x) & 3)
    by_y = ((first + y) & 3) * SIDE + ((second + x) & 3)
    return jnp.where(where[3] == 0, by_x, by_y)


CHUNK = 1024


def fetch(wq_ref, wkv_ref, held, sems):
    copies = []
    for i in range(wq_ref.shape[1] // CHUNK):
        part = wq_ref.at[:, pl.ds(i * CHUNK, CHUNK)]
        copies.append(pltpu.make_async_copy(part, held.at[i], sems.at[i]))
    copies.append(pltpu.make_async_copy(wkv_ref, held.at[len(copies)], sems.at[len(copies)]))
    for copy in copies:
        copy.start()
    return copies


def project_kernel(firsts, where, gain_ref, wq_ref, wkv_ref, *refs):
    count_outs = 2 * len(firsts)
    x_ref, far_ref, *given = refs[: -count_outs - 3]
    outs = refs[-count_outs - 3 : -3]
    scaled, held, sems = refs[-3:]
    copies = fetch(wq_ref, wkv_ref, held, sems)
    half, depth = x_ref.shape
    count = 2 * half // (SIDE * SIDE)
    width = CHUNK * len(copies)
    gain = gain_ref[...].astype(F32)
    own = where[3]
    outside = where[2] == 0
    for n, first in enumerate(firsts):
        for second in range(SIDE):
            at = rollout_of(where, first, second) * count
            here = at // half == own
            at = pl.multiple_of(at % half, count)
            x = jnp.where(here, x_ref[pl.ds(at, count), :], far_ref[pl.ds(at, count), :])
            if given:
                own_rows, far_rows = given[0][pl.ds(at, count), :], given[1][pl.ds(at, count), :]
                x = jnp.where(outside, jnp.where(here, own_rows, far_rows), x)
            x = x.astype(F32)
            square = x * x
            sums = square[:, :SUMS]
            for low in range(SUMS, depth, SUMS):
                sums = sums + square[:, low : low + SUMS]
            low = (n * SIDE + second) * count
            scaled[low : low + count, :] = (x * gain).astype(BF16)
            low = second % 2 * count
            outs[2 * n + second // 2][low : low + count, width:] = sums.astype(BF16)
    value = scaled[...]
    for i, copy in enumerate(copies):
        copy.wait()
        product = dot(value, held[i]).astype(BF16)
        for n, out in enumerate(outs):
            low = n * 2 * count
            out[:, i * CHUNK : (i + 1) * CHUNK] = product[low : low + 2 * count]


def project(firsts, where, inputs, gain, wq, wkv):
    half, depth = inputs[0].shape
    tokens = 2 * half // SIDE
    inner = wq.shape[1] + wkv.shape[1]
    chunks = inner // CHUNK
    block = jax.ShapeDtypeStruct((tokens // 2, inner + SUMS), BF16)
    outs = pl.pallas_call(
        lambda *refs: project_kernel(firsts, *refs),
        in_specs=[SMEM, VMEM, HBM, HBM] + [VMEM] * len(inputs),
        out_specs=[VMEM] * (2 * len(firsts)),
        out_shape=[block] * (2 * len(firsts)),
        scratch_shapes=[
            pltpu.VMEM((len(firsts) * tokens, depth), BF16),
            pltpu.VMEM((chunks, depth, CHUNK), BF16),
            pltpu.SemaphoreType.DMA((chunks,)),
        ],
        compiler_params=params(10),
        cost_estimate=pl.CostEstimate(
            flops=2 * len(firsts) * tokens * depth * inner,
            bytes_accessed=6 * 2**20,
            transcendentals=0,
        ),
        name="project_lead" if len(firsts) == 1 else "project_rest",
    )(where, gain, wq, wkv, *inputs)
    return {first: tuple(outs[2 * n : 2 * n + 2]) for n, first in enumerate(firsts)}


def add(*blocks):
    total = blocks[0].astype(F32)
    for block in blocks[1:]:
        total = total + block.astype(F32)
    return total.astype(BF16)


def first_sum(outs):
    (o0a, o0b), (o1a, o1b), (o2a, o2b), (o3a, o3b) = [outs[d] for d in range(SIDE)]
    passing_a = ring(o2a, FIRST, 1)
    passing_b = ring(o2b, FIRST, SIDE - 1)
    from_behind_b = ring(o1b, FIRST, 1)
    from_ahead_a = ring(o3a, FIRST, SIDE - 1)
    from_behind_a = ring(add(o1a, passing_a), FIRST, 1)
    from_ahead_b = ring(add(o3b, passing_b), FIRST, SIDE - 1)
    return (o0a, from_ahead_a, from_behind_a), (o0b, from_behind_b, from_ahead_b)


def combine(halves):
    outs = []
    for blocks in halves:
        count = blocks[0].shape[0] // 2
        for low in (0, count):
            outs.append(add(*[block[low : low + count] for block in blocks]))
    return outs


def helpers(heads, parts, cos_ref, sin_ref, kvb_ref):
    kv_width = heads * HD
    query_width = 4 * kv_width

    def columns(low, high):
        total = parts[0][:, low:high].astype(F32)
        for part in parts[1:]:
            total = total + part[:, low:high].astype(F32)
        return total

    width = parts[0].shape[1]
    squares = jnp.sum(columns(width - SUMS, width), axis=1, keepdims=True)
    scale = lax.rsqrt(squares / D + 1e-06)
    cosine = cos_ref[...]
    sine = sin_ref[...]

    def rotate(values):
        return (values * cosine + pltpu.roll(values, HD // 2, 1) * sine).astype(BF16)

    def new_head(head):
        low = head * HD
        key = columns(query_width + low, query_width + low + HD) * scale
        key = rotate(key + kvb_ref[0:1, low : low + HD].astype(F32))
        low_value = query_width + kv_width + low
        val = columns(low_value, low_value + HD) * scale
        return key, (val + kvb_ref[1:2, low : low + HD].astype(F32)).astype(BF16)

    return columns, scale, rotate, new_head


def put_rows(rows, heads, head, key, val):
    count = key.shape[0]
    rows[pl.ds(2 * head, count, stride=2 * heads), :] = key.astype(F32)
    rows[pl.ds(2 * head + 1, count, stride=2 * heads), :] = val.astype(F32)


def attend_kernel(heads, past, *refs):
    (length_ref, p0, p1, p2, p3, cos_ref, sin_ref, qb_ref, kvb_ref, cache_ref) = refs[:10]
    if past:
        old_keys, old_vals = refs[10:12]
    out_ref, key_ref, val_ref, page_ref, held, sems, rows = refs[-7:]
    length = length_ref[0]
    copies = []
    for head in range(heads):
        for kind in range(2):
            part = cache_ref.at[:, pl.ds((kind * heads + head) * HD, HD)]
            at = 2 * head + kind
            copies.append(pltpu.make_async_copy(part, held.at[at], sems.at[at]))
            copies[-1].start()
    count = p0.shape[0]
    kv_width = heads * HD
    query_width = 4 * kv_width
    columns, scale, rotate, new_head = helpers(
        heads, (p0, p1, p2, p3), cos_ref, sin_ref, kvb_ref
    )

    context = cache_ref.shape[0]
    seen = lax.broadcasted_iota(jnp.int32, (1, context), 1) < length
    shape = (4 * count, past + count)
    token = lax.broadcasted_iota(jnp.int32, shape, 0) % count
    causal = lax.broadcasted_iota(jnp.int32, shape, 1) <= token + past
    factor = 1.0 / math.sqrt(HD)

    def scores(q, k):
        return lax.dot_general(q, k, (((1,), (1,)), ((), ())), preferred_element_type=F32)

    for head in range(heads):
        low = head * HD
        key, val = new_head(head)
        put_rows(rows, heads, head, key, val)
        key_ref[:, low : low + HD] = key
        val_ref[:, low : low + HD] = val
        if past:
            key = jnp.concatenate([old_keys[:, low : low + HD], key], axis=0)
            val = jnp.concatenate([old_vals[:, low : low + HD], val], axis=0)
        group = []
        for g in range(4):
            at = (head * 4 + g) * HD
            query = columns(at, at + HD) * scale + qb_ref[0:1, at : at + HD].astype(F32)
            group.append(rotate(query))
        query = jnp.concatenate(group, axis=0)
        copies[2 * head].wait()
        cached = jnp.where(seen, scores(query, held[2 * head]), -1e30)
        recent = jnp.where(causal, scores(query, key), -1e30)
        peak = jnp.maximum(
            jnp.max(cached, axis=1, keepdims=True), jnp.max(recent, axis=1, keepdims=True)
        )
        cached = jnp.exp((cached - peak) * factor)
        recent = jnp.exp((recent - peak) * factor)
        total = jnp.sum(cached, axis=1, keepdims=True) + jnp.sum(recent, axis=1, keepdims=True)
        copies[2 * head + 1].wait()
        mixed = dot(cached.astype(BF16), held[2 * head + 1]) + dot(recent.astype(BF16), val)
        mixed = (mixed / total).astype(BF16)
        for g in range(4):
            at = (head * 4 + g) * HD
            out_ref[:, at : at + HD] = mixed[g * count : (g + 1) * count]
    page_ref[...] = rows[...].astype(BF16)


def page_kernel(heads, p0, p1, p2, p3, cos_ref, sin_ref, kvb_ref, page_ref, rows):
    new_head = helpers(heads, (p0, p1, p2, p3), cos_ref, sin_ref, kvb_ref)[3]
    for head in range(heads):
        put_rows(rows, heads, head, *new_head(head))
    page_ref[...] = rows[...].astype(BF16)


def new_page(parts, cosine, sine, keyval_bias):
    heads = keyval_bias.shape[1] // HD
    page = (2 * heads * parts[0].shape[0], HD)
    return pl.pallas_call(
        lambda *refs: page_kernel(heads, *refs),
        in_specs=[VMEM] * 7,
        out_specs=VMEM,
        out_shape=jax.ShapeDtypeStruct(page, BF16),
        scratch_shapes=[pltpu.VMEM(page, F32)],
        compiler_params=params(4),
        cost_estimate=pl.CostEstimate(flops=2**20, bytes_accessed=2**20, transcendentals=0),
        name="new_page",
    )(*parts, cosine, sine, keyval_bias)


def attend(length, parts, cosine, sine, query_bias, keyval_bias, cache, olds):
    kv_width = keyval_bias.shape[1]
    heads = kv_width // HD
    count = parts[0].shape[0]
    past = olds[0].shape[0] if olds else 0
    operands = [*parts, cosine, sine, query_bias, keyval_bias, cache, *olds]
    keys = cache.shape[0] + past + count
    return pl.pallas_call(
        lambda *refs: attend_kernel(heads, past, *refs),
        in_specs=[SMEM] + [VMEM] * 8 + [HBM] + [VMEM] * len(olds),
        out_specs=[VMEM] * 4,
        out_shape=[
            jax.ShapeDtypeStruct((count, 4 * kv_width), BF16),
            jax.ShapeDtypeStruct((count, kv_width), BF16),
            jax.ShapeDtypeStruct((count, kv_width), BF16),
            jax.ShapeDtypeStruct((2 * heads * count, HD), BF16),
        ],
        scratch_shapes=[
            pltpu.VMEM((2 * heads, cache.shape[0], HD), BF16),
            pltpu.SemaphoreType.DMA((2 * heads,)),
            pltpu.VMEM((2 * heads * count, HD), F32),
        ],
        compiler_params=params(8),
        cost_estimate=pl.CostEstimate(
            flops=16 * count * keys * kv_width,
            bytes_accessed=4 * 2**20,
            transcendentals=4 * count * heads * keys,
        ),
        name="attend",
    )(length, *operands)


def join_kernel(*refs):
    out = refs[-1]
    count = refs[0].shape[0]
    for i, block in enumerate(refs[:-1]):
        out[i * count : (i + 1) * count, :] = block[...]


def join(blocks):
    count, width = blocks[0].shape
    return pl.pallas_call(
        join_kernel,
        in_specs=[VMEM] * len(blocks),
        out_specs=VMEM,
        out_shape=jax.ShapeDtypeStruct((len(blocks) * count, width), BF16),
        compiler_params=params(4),
        cost_estimate=pl.CostEstimate(flops=0, bytes_accessed=2**20, transcendentals=0),
        name="join",
    )(*blocks)


def gate_kernel(block_ref, ready_ref, out_ref):
    del block_ref, ready_ref, out_ref


def gate(block, ready):
    anywhere = pl.BlockSpec(memory_space=pl.ANY)
    return pl.pallas_call(
        gate_kernel,
        in_specs=[anywhere, anywhere],
        out_specs=anywhere,
        out_shape=jax.ShapeDtypeStruct(block.shape, block.dtype),
        input_output_aliases={0: 0},
        compiler_params=params(4),
        name="gate",
    )(block, ready)


def place_kernel(where, *refs):
    blocks = refs[:-2]
    mine_ref, other_ref = refs[-2:]
    half = mine_ref.shape[0]
    count = blocks[0].shape[0] // SIDE
    own = where[3] * half
    for second, block in enumerate(blocks):
        for first in range(SIDE):
            at = rollout_of(where, first, second) * count - own
            here = (at >= 0) & (at < half)
            value = block[first * count : (first + 1) * count, :]

            @pl.when(here)
            def _():
                mine_ref[pl.ds(pl.multiple_of(at, count), count), :] = value

            @pl.when(jnp.logical_not(here))
            def _():
                there = jnp.where(at < 0, at + half, at - half)
                other_ref[pl.ds(pl.multiple_of(there, count), count), :] = value


def place(where, blocks):
    tokens, width = blocks[0].shape
    return pl.pallas_call(
        place_kernel,
        in_specs=[SMEM] + [VMEM] * len(blocks),
        out_specs=[VMEM] * 2,
        out_shape=[jax.ShapeDtypeStruct((2 * tokens, width), BF16)] * 2,
        compiler_params=params(8),
        cost_estimate=pl.CostEstimate(flops=0, bytes_accessed=2**20, transcendentals=0),
        name="place",
    )(where, *blocks)


def merge_kernel(stacked, where, active_ref, mine_ref, theirs_ref, x_ref, *refs):
    given, out_ref = refs[:-1], refs[-1]
    active = active_ref[where[2]].astype(F32)
    x = x_ref[...]
    if given:
        x = jnp.where(where[2] == 0, given[0][...], x)
    mixed = mine_ref[...].astype(F32) + theirs_ref[...].astype(F32)
    done = (x.astype(F32) + active * mixed).astype(BF16)
    if stacked:
        for i, before in enumerate(given[1:]):
            out_ref[i] = before[...]
        out_ref[len(given) - 1] = done
    else:
        out_ref[...] = done


def merge(where, active, mine, theirs, inputs, before=()):
    operands = [mine, theirs, *inputs, *before]
    shape = mine.shape
    if before:
        shape = (len(before) + 1,) + shape
    return pl.pallas_call(
        lambda *refs: merge_kernel(bool(before), *refs),
        in_specs=[SMEM, SMEM] + [VMEM] * len(operands),
        out_specs=VMEM,
        out_shape=jax.ShapeDtypeStruct(shape, BF16),
        compiler_params=params(8),
        cost_estimate=pl.CostEstimate(flops=2**20, bytes_accessed=2**20, transcendentals=0),
        name="merge",
    )(where, active, *operands)


def ship_kernel(table_ref, resident_ref, out_ref, held, arrival, sems):
    start = table_ref[table_ref.shape[0] - 1]
    whole = pltpu.make_async_copy(resident_ref, held, arrival)
    whole.start()
    whole.wait()

    def each(act):
        def body(p, carry):
            @pl.when(p < start)
            def _():
                act(held.at[p], p)

            return carry

        lax.fori_loop(0, held.shape[0], body, 0)

    def copy(source, p):
        return pltpu.make_async_copy(source, out_ref.at[table_ref[p]], sems.at[p])

    each(lambda source, p: copy(source, p).start())
    each(lambda source, p: copy(source, p).wait())


def ship(table, resident, count):
    return pl.pallas_call(
        ship_kernel,
        in_specs=[SMEM, HBM],
        out_specs=HBM,
        out_shape=jax.ShapeDtypeStruct((count,) + resident.shape[1:], BF16),
        scratch_shapes=[
            pltpu.VMEM(resident.shape, BF16),
            pltpu.SemaphoreType.DMA,
            pltpu.SemaphoreType.DMA((table.shape[0] - 1,)),
        ],
        compiler_params=params(40),
        cost_estimate=pl.CostEstimate(flops=0, bytes_accessed=5 * 2**20, transcendentals=0),
        name="ship",
    )(table, resident)


def ship_last_kernel(table_ref, f0, f1, f2, given_ref, out_ref, sems):
    start = table_ref[table_ref.shape[0] - 1]
    copies = [
        pltpu.make_async_copy(page, out_ref.at[table_ref[start + i]], sems.at[i])
        for i, page in enumerate((f0, f1, f2))
    ]
    for copy in copies:
        copy.start()
    for copy in copies:
        copy.wait()


def ship_last(table, fresh, given):
    return pl.pallas_call(
        ship_last_kernel,
        in_specs=[SMEM] + [VMEM] * BLOCKS + [HBM],
        out_specs=HBM,
        out_shape=jax.ShapeDtypeStruct(given.shape, BF16),
        scratch_shapes=[pltpu.SemaphoreType.DMA((BLOCKS,))],
        input_output_aliases={1 + BLOCKS: 0},
        compiler_params=params(40),
        cost_estimate=pl.CostEstimate(flops=0, bytes_accessed=2**18, transcendentals=0),
        name="ship_last",
    )(table, *fresh, given)


def store_kernel(table_ref, arrived_ref, pool_ref, held, reads, writes):
    slots = pool_ref.shape[0]

    def read(q):
        source = jnp.maximum(table_ref[q], 0)
        return pltpu.make_async_copy(arrived_ref.at[source], held.at[q], reads.at[q])

    def write(q):
        return pltpu.make_async_copy(held.at[q], pool_ref.at[q], writes.at[q])

    def each(act):
        def body(q, carry):
            act(q)
            return carry

        lax.fori_loop(0, slots, body, 0)

    def begin(q):
        @pl.when(table_ref[q] >= 0)
        def _():
            read(q).start()

    def turn(q):
        @pl.when(table_ref[q] >= 0)
        def _():
            read(q).wait()

        @pl.when(table_ref[q] < 0)
        def _():
            held[q] = jnp.zeros(held.shape[1:], BF16)

        write(q).start()

    each(begin)
    each(turn)
    each(lambda q: write(q).wait())


def store(table, arrived, slots):
    return pl.pallas_call(
        store_kernel,
        in_specs=[SMEM, HBM],
        out_specs=HBM,
        out_shape=jax.ShapeDtypeStruct((slots,) + arrived.shape[1:], BF16),
        scratch_shapes=[
            pltpu.VMEM((slots,) + arrived.shape[1:], BF16),
            pltpu.SemaphoreType.DMA((slots,)),
            pltpu.SemaphoreType.DMA((slots,)),
        ],
        compiler_params=params(6),
        cost_estimate=pl.CostEstimate(flops=0, bytes_accessed=5 * 2**20, transcendentals=0),
        name="store",
    )(table, arrived)


def local(
    entering,
    arriving,
    w_query,
    w_keyval,
    w_out,
    query_bias,
    keyval_bias,
    norm_gain,
    resident_kv,
    resumed_pages,
    section_active,
    block_table,
):
    section_count = lax.axis_size("section")
    y = lax.axis_index("y")
    x = lax.axis_index("x")
    section = lax.axis_index("section")
    tensor = lax.axis_index("tensor")
    rollout = y * SIDE + x
    roll_count = SIDE * SIDE
    kv_width = w_keyval.shape[3]
    wq = w_query[0]
    wkv = w_keyval[0].reshape(w_keyval.shape[1], 2 * kv_width)
    w_mix = w_out[0]
    length = resumed_pages[rollout] * PAGE + (section_count - 1 - section) * BLOCK

    where = jnp.stack([y, x, section, tensor]).astype(jnp.int32)

    half = HD // 2
    freq = jnp.power(F32(1000000.0), -(jnp.arange(half, dtype=F32) * (2.0 / HD)))
    positions = length + jnp.arange(BLOCKS * BLOCK, dtype=jnp.int32)
    angle = positions.astype(F32)[:, None] * freq[None, :]
    cosine = jnp.concatenate([jnp.cos(angle), jnp.cos(angle)], axis=1)
    sine = jnp.concatenate([-jnp.sin(angle), jnp.sin(angle)], axis=1)

    resident = resident_kv[0, 0]
    keyval_shift = keyval_bias[0]
    swap = [(0, 1), (1, 0)]
    relay = [(i, i + 1) for i in range(section_count - 1)]

    dest_count = roll_count * section_count
    slots = block_table.shape[2]
    routing = block_table.reshape(dest_count, slots, 2)
    targets = routing[:, :, 0]
    slot_ids = routing[:, :, 1]
    own = rollout * section_count + section

    def order_of(device):
        return device % section_count * roll_count + device // section_count

    sources = jnp.arange(dest_count, dtype=jnp.int32)
    source_pages = (
        resumed_pages[:, None]
        + (section_count - 1 - jnp.arange(section_count, dtype=jnp.int32))[None, :]
        + BLOCKS
    )
    live_pages = jnp.where(section_active[None, :] > 0, source_pages, 0).reshape(-1)
    page_ids = jnp.arange(slots, dtype=jnp.int32)
    mine = (targets == own) & (page_ids[None, :] < live_pages[:, None])
    hit = mine[:, :, None] & (slot_ids[:, :, None] == page_ids)
    origin = jnp.max(jnp.where(hit, order_of(sources)[:, None, None], -1), axis=(0, 1))

    def table_of(block_table):
        slots_of = order_of(block_table.reshape(dest_count, slots, 2)[own, :, 0])
        return jnp.concatenate([slots_of, (length // PAGE)[None]]).astype(jnp.int32)


    heads = kv_width // HD
    pages = resident.reshape(-1, 2, heads, HD).swapaxes(1, 2).reshape(-1, PAGE * 2 * heads, HD)

    fresh_keys = []
    fresh_vals = []
    fresh = []
    results = []
    for step in range(BLOCKS):
        last = step == BLOCKS - 1
        if step == 0:
            inputs = [entering[0], lax.ppermute(entering[0], "tensor", swap)]
        else:
            handed = lax.ppermute(results[-1], "section", relay)
            if step == 1:
                slots_ahead, _ = lax.optimization_barrier((early[-1], results[-1]))
                outgoing = ship(slots_ahead, pages, dest_count)
                handed, outgoing = lax.optimization_barrier((handed, outgoing))
            inputs = [handed, lax.ppermute(handed, "tensor", swap)]
            inputs += early[2 * step - 2 : 2 * step]
        outs = project((2,), where, inputs, norm_gain, wq, wkv)
        outs.update(project((1, 3, 0), where, inputs, norm_gain, wq, wkv))
        if step == 0:
            late, given, table, outs[0] = lax.optimization_barrier(
                (resident, arriving, block_table, outs[0])
            )
            table = table_of(table)
            cache = late.reshape(resident.shape[0], 2 * kv_width)
            given_far = lax.ppermute(given, "tensor", swap)
            early = [given[0], given_far[0], given[1], given_far[1], table]
        outs = combine(first_sum(outs))
        if step == 0:
            outs, early = lax.optimization_barrier((outs, early))
        parts = [outs[0]] + [ring(outs[d], SECOND, d) for d in (2, 1, 3)]
        at = slice(step * BLOCK, (step + 1) * BLOCK)
        if last:
            fresh.append(new_page(parts, cosine[at], sine[at], keyval_shift))
            outgoing = ship_last(early[-1], fresh, outgoing)
            arrived = lax.all_to_all(outgoing, ("section",) + ROLL, 0, 0, tiled=True)
            pool = store(origin, arrived, slots)
        olds = []
        if fresh_keys:
            olds = [jnp.concatenate(fresh_keys), jnp.concatenate(fresh_vals)]
        attended, key, val, page = attend(
            length[None],
            parts,
            cosine[at],
            sine[at],
            query_bias,
            keyval_shift,
            cache,
            olds,
        )
        fresh_keys.append(key)
        fresh_vals.append(val)
        fresh.append(page)
        ahead, across, behind = [ring(attended, FIRST, SIDE - d) for d in range(1, SIDE)]
        gathered = join([attended, ahead, across, behind])
        gathered = gate(gathered, lax.ppermute(gathered[:16, :HD], "tensor", swap))
        late_mix = w_mix
        blocks = [gathered] + [ring(gathered, SECOND, SIDE - d) for d in range(1, SIDE)]
        if last:
            late_mix, pool = lax.optimization_barrier((w_mix, pool))
        mine, other = place(where, [dot(block, late_mix).astype(BF16) for block in blocks])
        theirs = lax.ppermute(other, "tensor", swap)
        kept = inputs[::2]
        results.append(merge(where, section_active, mine, theirs, kept, results if last else ()))
    section_out = results[-1][None]

    pool = pool.reshape(slots * PAGE, heads, 2, HD).swapaxes(1, 2)
    return section_out, pool.reshape(1, 1, slots, PAGE, 2, kv_width)


def solution(mesh):
    split = Mesh(mesh.devices.reshape(SIDE, SIDE, mesh.shape["section"], 2), ALL)
    in_specs = (
        P("section", "tensor", ROLL),
        P(None, "tensor", ROLL),
        P("section", ROLL, "tensor"),
        P("section", ROLL, None, "tensor"),
        P("section", "tensor", ROLL),
        P("section", "tensor"),
        P("section", None, "tensor"),
        P("section", ROLL),
        P(ROLL, "section", None, None, "tensor"),
        P(),
        P(),
        P(),
    )
    out_specs = (
        P("section", None, "tensor", ROLL),
        P(ROLL, "section", None, None, None, "tensor"),
    )
    return jax.shard_map(
        local, mesh=split, in_specs=in_specs, out_specs=out_specs, check_vma=False
    )
```

```python
import math

import jax
import jax.numpy as jnp
from jax import lax
from jax.experimental import pallas as pl
from jax.experimental.pallas import tpu as pltpu
from jax.sharding import Mesh, PartitionSpec as P

D = 8192
HD = 128
BLOCK = 32
BLOCKS = 3
PAGE = 32
SIDE = 4
SUMS = 128
ROLL = ("y", "x")
ALL = ("y", "x", "section", "tensor")
F32 = jnp.float32
BF16 = jnp.bfloat16


HBM = pl.BlockSpec(memory_space=pltpu.HBM)
VMEM = pl.BlockSpec(memory_space=pltpu.VMEM)
SMEM = pl.BlockSpec(memory_space=pltpu.SMEM)


def dot(a, b):
    return jnp.dot(a, b, preferred_element_type=F32)


def params(megabytes):
    return pltpu.CompilerParams(vmem_limit_bytes=megabytes * 1024 * 1024)


def ring_routes(phase):
    routes = {}
    for shift in range(1, SIDE):
        route = []
        for y in range(SIDE):
            for x in range(SIDE):
                for s in range(SIDE):
                    for t in range(2):
                        along_x = t == phase
                        ty, tx = (y, (x + shift) % SIDE) if along_x else ((y + shift) % SIDE, x)
                        route.append(
                            (
                                ((y * SIDE + x) * SIDE + s) * 2 + t,
                                ((ty * SIDE + tx) * SIDE + s) * 2 + t,
                            )
                        )
        routes[shift] = route
    return routes


FIRST = ring_routes(0)
SECOND = ring_routes(1)


def ring(block, routes, shift):
    return lax.ppermute(block, ALL, routes[shift])


def rollout_of(where, first, second):
    y, x = where[0], where[1]
    by_x = ((second + y) & 3) * SIDE + ((first + x) & 3)
    by_y = ((first + y) & 3) * SIDE + ((second + x) & 3)
    return jnp.where(where[3] == 0, by_x, by_y)


CHUNK = 1024


def fetch(wq_ref, wkv_ref, held, sems):
    copies = []
    for i in range(wq_ref.shape[1] // CHUNK):
        part = wq_ref.at[:, pl.ds(i * CHUNK, CHUNK)]
        copies.append(pltpu.make_async_copy(part, held.at[i], sems.at[i]))
    copies.append(pltpu.make_async_copy(wkv_ref, held.at[len(copies)], sems.at[len(copies)]))
    for copy in copies:
        copy.start()
    return copies


def project_kernel(firsts, where, gain_ref, wq_ref, wkv_ref, *refs):
    count_outs = 2 * len(firsts)
    x_ref, far_ref, *given = refs[: -count_outs - 3]
    outs = refs[-count_outs - 3 : -3]
    scaled, held, sems = refs[-3:]
    copies = fetch(wq_ref, wkv_ref, held, sems)
    half, depth = x_ref.shape
    count = 2 * half // (SIDE * SIDE)
    width = CHUNK * len(copies)
    gain = gain_ref[...].astype(F32)
    own = where[3]
    outside = where[2] == 0
    for n, first in enumerate(firsts):
        for second in range(SIDE):
            at = rollout_of(where, first, second) * count
            here = at // half == own
            at = pl.multiple_of(at % half, count)
            x = jnp.where(here, x_ref[pl.ds(at, count), :], far_ref[pl.ds(at, count), :])
            if given:
                own_rows, far_rows = given[0][pl.ds(at, count), :], given[1][pl.ds(at, count), :]
                x = jnp.where(outside, jnp.where(here, own_rows, far_rows), x)
            x = x.astype(F32)
            square = x * x
            sums = square[:, :SUMS]
            for low in range(SUMS, depth, SUMS):
                sums = sums + square[:, low : low + SUMS]
            low = (n * SIDE + second) * count
            scaled[low : low + count, :] = (x * gain).astype(BF16)
            low = second % 2 * count
            outs[2 * n + second // 2][low : low + count, width:] = sums.astype(BF16)
    value = scaled[...]
    for i, copy in enumerate(copies):
        copy.wait()
        product = dot(value, held[i]).astype(BF16)
        for n, out in enumerate(outs):
            low = n * 2 * count
            out[:, i * CHUNK : (i + 1) * CHUNK] = product[low : low + 2 * count]


def project(firsts, where, inputs, gain, wq, wkv):
    half, depth = inputs[0].shape
    tokens = 2 * half // SIDE
    inner = wq.shape[1] + wkv.shape[1]
    chunks = inner // CHUNK
    block = jax.ShapeDtypeStruct((tokens // 2, inner + SUMS), BF16)
    outs = pl.pallas_call(
        lambda *refs: project_kernel(firsts, *refs),
        in_specs=[SMEM, VMEM, HBM, HBM] + [VMEM] * len(inputs),
        out_specs=[VMEM] * (2 * len(firsts)),
        out_shape=[block] * (2 * len(firsts)),
        scratch_shapes=[
            pltpu.VMEM((len(firsts) * tokens, depth), BF16),
            pltpu.VMEM((chunks, depth, CHUNK), BF16),
            pltpu.SemaphoreType.DMA((chunks,)),
        ],
        compiler_params=params(10),
        cost_estimate=pl.CostEstimate(
            flops=2 * len(firsts) * tokens * depth * inner,
            bytes_accessed=6 * 2**20,
            transcendentals=0,
        ),
        name="project_lead" if len(firsts) == 1 else "project_rest",
    )(where, gain, wq, wkv, *inputs)
    return {first: tuple(outs[2 * n : 2 * n + 2]) for n, first in enumerate(firsts)}


def add(*blocks):
    total = blocks[0].astype(F32)
    for block in blocks[1:]:
        total = total + block.astype(F32)
    return total.astype(BF16)


def first_sum(outs):
    (o0a, o0b), (o1a, o1b), (o2a, o2b), (o3a, o3b) = [outs[d] for d in range(SIDE)]
    passing_a = ring(o2a, FIRST, 1)
    passing_b = ring(o2b, FIRST, SIDE - 1)
    from_behind_b = ring(o1b, FIRST, 1)
    from_ahead_a = ring(o3a, FIRST, SIDE - 1)
    from_behind_a = ring(add(o1a, passing_a), FIRST, 1)
    from_ahead_b = ring(add(o3b, passing_b), FIRST, SIDE - 1)
    return (o0a, from_ahead_a, from_behind_a), (o0b, from_behind_b, from_ahead_b)


def combine(halves):
    outs = []
    for blocks in halves:
        count = blocks[0].shape[0] // 2
        for low in (0, count):
            outs.append(add(*[block[low : low + count] for block in blocks]))
    return outs


def helpers(heads, parts, cos_ref, sin_ref, kvb_ref):
    kv_width = heads * HD
    query_width = 4 * kv_width

    def columns(low, high):
        total = parts[0][:, low:high].astype(F32)
        for part in parts[1:]:
            total = total + part[:, low:high].astype(F32)
        return total

    width = parts[0].shape[1]
    squares = jnp.sum(columns(width - SUMS, width), axis=1, keepdims=True)
    scale = lax.rsqrt(squares / D + 1e-06)
    cosine = cos_ref[...]
    sine = sin_ref[...]

    def rotate(values):
        return (values * cosine + pltpu.roll(values, HD // 2, 1) * sine).astype(BF16)

    def new_head(head):
        low = head * HD
        key = columns(query_width + low, query_width + low + HD) * scale
        key = rotate(key + kvb_ref[0:1, low : low + HD].astype(F32))
        low_value = query_width + kv_width + low
        val = columns(low_value, low_value + HD) * scale
        return key, (val + kvb_ref[1:2, low : low + HD].astype(F32)).astype(BF16)

    return columns, scale, rotate, new_head


def put_rows(rows, heads, head, key, val):
    count = key.shape[0]
    rows[pl.ds(2 * head, count, stride=2 * heads), :] = key.astype(F32)
    rows[pl.ds(2 * head + 1, count, stride=2 * heads), :] = val.astype(F32)


def attend_kernel(heads, past, *refs):
    (length_ref, p0, p1, p2, p3, cos_ref, sin_ref, qb_ref, kvb_ref, cache_ref) = refs[:10]
    if past:
        old_keys, old_vals = refs[10:12]
    out_ref, key_ref, val_ref, page_ref, held, sems, rows = refs[-7:]
    length = length_ref[0]
    copies = []
    for head in range(heads):
        for kind in range(2):
            part = cache_ref.at[:, pl.ds((kind * heads + head) * HD, HD)]
            at = 2 * head + kind
            copies.append(pltpu.make_async_copy(part, held.at[at], sems.at[at]))
            copies[-1].start()
    count = p0.shape[0]
    kv_width = heads * HD
    query_width = 4 * kv_width
    columns, scale, rotate, new_head = helpers(
        heads, (p0, p1, p2, p3), cos_ref, sin_ref, kvb_ref
    )

    context = cache_ref.shape[0]
    seen = lax.broadcasted_iota(jnp.int32, (1, context), 1) < length
    shape = (4 * count, past + count)
    token = lax.broadcasted_iota(jnp.int32, shape, 0) % count
    causal = lax.broadcasted_iota(jnp.int32, shape, 1) <= token + past
    factor = 1.0 / math.sqrt(HD)

    def scores(q, k):
        return lax.dot_general(q, k, (((1,), (1,)), ((), ())), preferred_element_type=F32)

    for head in range(heads):
        low = head * HD
        key, val = new_head(head)
        put_rows(rows, heads, head, key, val)
        key_ref[:, low : low + HD] = key
        val_ref[:, low : low + HD] = val
        if past:
            key = jnp.concatenate([old_keys[:, low : low + HD], key], axis=0)
            val = jnp.concatenate([old_vals[:, low : low + HD], val], axis=0)
        group = []
        for g in range(4):
            at = (head * 4 + g) * HD
            query = columns(at, at + HD) * scale + qb_ref[0:1, at : at + HD].astype(F32)
            group.append(rotate(query))
        query = jnp.concatenate(group, axis=0)
        copies[2 * head].wait()
        cached = jnp.where(seen, scores(query, held[2 * head]), -1e30)
        recent = jnp.where(causal, scores(query, key), -1e30)
        peak = jnp.maximum(
            jnp.max(cached, axis=1, keepdims=True), jnp.max(recent, axis=1, keepdims=True)
        )
        cached = jnp.exp((cached - peak) * factor)
        recent = jnp.exp((recent - peak) * factor)
        total = jnp.sum(cached, axis=1, keepdims=True) + jnp.sum(recent, axis=1, keepdims=True)
        copies[2 * head + 1].wait()
        mixed = dot(cached.astype(BF16), held[2 * head + 1]) + dot(recent.astype(BF16), val)
        mixed = (mixed / total).astype(BF16)
        for g in range(4):
            at = (head * 4 + g) * HD
            out_ref[:, at : at + HD] = mixed[g * count : (g + 1) * count]
    page_ref[...] = rows[...].astype(BF16)


def page_kernel(heads, p0, p1, p2, p3, cos_ref, sin_ref, kvb_ref, page_ref, rows):
    new_head = helpers(heads, (p0, p1, p2, p3), cos_ref, sin_ref, kvb_ref)[3]
    for head in range(heads):
        put_rows(rows, heads, head, *new_head(head))
    page_ref[...] = rows[...].astype(BF16)


def new_page(parts, cosine, sine, keyval_bias):
    heads = keyval_bias.shape[1] // HD
    page = (2 * heads * parts[0].shape[0], HD)
    return pl.pallas_call(
        lambda *refs: page_kernel(heads, *refs),
        in_specs=[VMEM] * 7,
        out_specs=VMEM,
        out_shape=jax.ShapeDtypeStruct(page, BF16),
        scratch_shapes=[pltpu.VMEM(page, F32)],
        compiler_params=params(4),
        cost_estimate=pl.CostEstimate(flops=2**20, bytes_accessed=2**20, transcendentals=0),
        name="new_page",
    )(*parts, cosine, sine, keyval_bias)


def attend(length, parts, cosine, sine, query_bias, keyval_bias, cache, olds):
    kv_width = keyval_bias.shape[1]
    heads = kv_width // HD
    count = parts[0].shape[0]
    past = olds[0].shape[0] if olds else 0
    operands = [*parts, cosine, sine, query_bias, keyval_bias, cache, *olds]
    keys = cache.shape[0] + past + count
    return pl.pallas_call(
        lambda *refs: attend_kernel(heads, past, *refs),
        in_specs=[SMEM] + [VMEM] * 8 + [HBM] + [VMEM] * len(olds),
        out_specs=[VMEM] * 4,
        out_shape=[
            jax.ShapeDtypeStruct((count, 4 * kv_width), BF16),
            jax.ShapeDtypeStruct((count, kv_width), BF16),
            jax.ShapeDtypeStruct((count, kv_width), BF16),
            jax.ShapeDtypeStruct((2 * heads * count, HD), BF16),
        ],
        scratch_shapes=[
            pltpu.VMEM((2 * heads, cache.shape[0], HD), BF16),
            pltpu.SemaphoreType.DMA((2 * heads,)),
            pltpu.VMEM((2 * heads * count, HD), F32),
        ],
        compiler_params=params(8),
        cost_estimate=pl.CostEstimate(
            flops=16 * count * keys * kv_width,
            bytes_accessed=4 * 2**20,
            transcendentals=4 * count * heads * keys,
        ),
        name="attend",
    )(length, *operands)


def join_kernel(*refs):
    out = refs[-1]
    count = refs[0].shape[0]
    for i, block in enumerate(refs[:-1]):
        out[i * count : (i + 1) * count, :] = block[...]


def join(blocks):
    count, width = blocks[0].shape
    return pl.pallas_call(
        join_kernel,
        in_specs=[VMEM] * len(blocks),
        out_specs=VMEM,
        out_shape=jax.ShapeDtypeStruct((len(blocks) * count, width), BF16),
        compiler_params=params(4),
        cost_estimate=pl.CostEstimate(flops=0, bytes_accessed=2**20, transcendentals=0),
        name="join",
    )(*blocks)


def gate_kernel(block_ref, ready_ref, out_ref):
    del block_ref, ready_ref, out_ref


def gate(block, ready):
    anywhere = pl.BlockSpec(memory_space=pl.ANY)
    return pl.pallas_call(
        gate_kernel,
        in_specs=[anywhere, anywhere],
        out_specs=anywhere,
        out_shape=jax.ShapeDtypeStruct(block.shape, block.dtype),
        input_output_aliases={0: 0},
        compiler_params=params(4),
        name="gate",
    )(block, ready)


def place_kernel(where, *refs):
    blocks = refs[:-2]
    mine_ref, other_ref = refs[-2:]
    half = mine_ref.shape[0]
    count = blocks[0].shape[0] // SIDE
    own = where[3] * half
    for second, block in enumerate(blocks):
        for first in range(SIDE):
            at = rollout_of(where, first, second) * count - own
            here = (at >= 0) & (at < half)
            value = block[first * count : (first + 1) * count, :]

            @pl.when(here)
            def _():
                mine_ref[pl.ds(pl.multiple_of(at, count), count), :] = value

            @pl.when(jnp.logical_not(here))
            def _():
                there = jnp.where(at < 0, at + half, at - half)
                other_ref[pl.ds(pl.multiple_of(there, count), count), :] = value


def place(where, blocks):
    tokens, width = blocks[0].shape
    return pl.pallas_call(
        place_kernel,
        in_specs=[SMEM] + [VMEM] * len(blocks),
        out_specs=[VMEM] * 2,
        out_shape=[jax.ShapeDtypeStruct((2 * tokens, width), BF16)] * 2,
        compiler_params=params(8),
        cost_estimate=pl.CostEstimate(flops=0, bytes_accessed=2**20, transcendentals=0),
        name="place",
    )(where, *blocks)


def merge_kernel(stacked, where, active_ref, mine_ref, theirs_ref, x_ref, *refs):
    given, out_ref = refs[:-1], refs[-1]
    active = active_ref[where[2]].astype(F32)
    x = x_ref[...]
    if given:
        x = jnp.where(where[2] == 0, given[0][...], x)
    mixed = mine_ref[...].astype(F32) + theirs_ref[...].astype(F32)
    done = (x.astype(F32) + active * mixed).astype(BF16)
    if stacked:
        for i, before in enumerate(given[1:]):
            out_ref[i] = before[...]
        out_ref[len(given) - 1] = done
    else:
        out_ref[...] = done


def merge(where, active, mine, theirs, inputs, before=()):
    operands = [mine, theirs, *inputs, *before]
    shape = mine.shape
    if before:
        shape = (len(before) + 1,) + shape
    return pl.pallas_call(
        lambda *refs: merge_kernel(bool(before), *refs),
        in_specs=[SMEM, SMEM] + [VMEM] * len(operands),
        out_specs=VMEM,
        out_shape=jax.ShapeDtypeStruct(shape, BF16),
        compiler_params=params(8),
        cost_estimate=pl.CostEstimate(flops=2**20, bytes_accessed=2**20, transcendentals=0),
        name="merge",
    )(where, active, *operands)


def ship_kernel(table_ref, resident_ref, out_ref, held, arrival, sems):
    start = table_ref[table_ref.shape[0] - 1]
    whole = pltpu.make_async_copy(resident_ref, held, arrival)
    whole.start()
    whole.wait()

    def each(act):
        def body(p, carry):
            @pl.when(p < start)
            def _():
                act(held.at[p], p)

            return carry

        lax.fori_loop(0, held.shape[0], body, 0)

    def copy(source, p):
        return pltpu.make_async_copy(source, out_ref.at[table_ref[p]], sems.at[p])

    each(lambda source, p: copy(source, p).start())
    each(lambda source, p: copy(source, p).wait())


def ship(table, resident, count):
    return pl.pallas_call(
        ship_kernel,
        in_specs=[SMEM, HBM],
        out_specs=HBM,
        out_shape=jax.ShapeDtypeStruct((count,) + resident.shape[1:], BF16),
        scratch_shapes=[
            pltpu.VMEM(resident.shape, BF16),
            pltpu.SemaphoreType.DMA,
            pltpu.SemaphoreType.DMA((table.shape[0] - 1,)),
        ],
        compiler_params=params(61),
        cost_estimate=pl.CostEstimate(flops=0, bytes_accessed=5 * 2**20, transcendentals=0),
        name="ship",
    )(table, resident)


def ship_last_kernel(table_ref, f0, f1, f2, given_ref, out_ref, sems):
    start = table_ref[table_ref.shape[0] - 1]
    copies = [
        pltpu.make_async_copy(page, out_ref.at[table_ref[start + i]], sems.at[i])
        for i, page in enumerate((f0, f1, f2))
    ]
    for copy in copies:
        copy.start()
    for copy in copies:
        copy.wait()


def ship_last(table, fresh, given):
    return pl.pallas_call(
        ship_last_kernel,
        in_specs=[SMEM] + [VMEM] * BLOCKS + [HBM],
        out_specs=HBM,
        out_shape=jax.ShapeDtypeStruct(given.shape, BF16),
        scratch_shapes=[pltpu.SemaphoreType.DMA((BLOCKS,))],
        input_output_aliases={1 + BLOCKS: 0},
        compiler_params=params(61),
        cost_estimate=pl.CostEstimate(flops=0, bytes_accessed=2**18, transcendentals=0),
        name="ship_last",
    )(table, *fresh, given)


def store_kernel(table_ref, arrived_ref, pool_ref, held, reads, writes):
    slots = pool_ref.shape[0]

    def read(q):
        source = jnp.maximum(table_ref[q], 0)
        return pltpu.make_async_copy(arrived_ref.at[source], held.at[q], reads.at[q])

    def write(q):
        return pltpu.make_async_copy(held.at[q], pool_ref.at[q], writes.at[q])

    def each(act):
        def body(q, carry):
            act(q)
            return carry

        lax.fori_loop(0, slots, body, 0)

    def begin(q):
        @pl.when(table_ref[q] >= 0)
        def _():
            read(q).start()

    def turn(q):
        @pl.when(table_ref[q] >= 0)
        def _():
            read(q).wait()

        @pl.when(table_ref[q] < 0)
        def _():
            held[q] = jnp.zeros(held.shape[1:], BF16)

        write(q).start()

    each(begin)
    each(turn)
    each(lambda q: write(q).wait())


def store(table, arrived, slots):
    return pl.pallas_call(
        store_kernel,
        in_specs=[SMEM, HBM],
        out_specs=HBM,
        out_shape=jax.ShapeDtypeStruct((slots,) + arrived.shape[1:], BF16),
        scratch_shapes=[
            pltpu.VMEM((slots,) + arrived.shape[1:], BF16),
            pltpu.SemaphoreType.DMA((slots,)),
            pltpu.SemaphoreType.DMA((slots,)),
        ],
        compiler_params=params(6),
        cost_estimate=pl.CostEstimate(flops=0, bytes_accessed=5 * 2**20, transcendentals=0),
        name="store",
    )(table, arrived)


def local(
    entering,
    arriving,
    w_query,
    w_keyval,
    w_out,
    query_bias,
    keyval_bias,
    norm_gain,
    resident_kv,
    resumed_pages,
    section_active,
    block_table,
):
    section_count = lax.axis_size("section")
    y = lax.axis_index("y")
    x = lax.axis_index("x")
    section = lax.axis_index("section")
    tensor = lax.axis_index("tensor")
    rollout = y * SIDE + x
    roll_count = SIDE * SIDE
    kv_width = w_keyval.shape[3]
    wq = w_query[0]
    wkv = w_keyval[0].reshape(w_keyval.shape[1], 2 * kv_width)
    w_mix = w_out[0]
    length = resumed_pages[rollout] * PAGE + (section_count - 1 - section) * BLOCK

    where = jnp.stack([y, x, section, tensor]).astype(jnp.int32)

    half = HD // 2
    freq = jnp.power(F32(1000000.0), -(jnp.arange(half, dtype=F32) * (2.0 / HD)))
    positions = length + jnp.arange(BLOCKS * BLOCK, dtype=jnp.int32)
    angle = positions.astype(F32)[:, None] * freq[None, :]
    cosine = jnp.concatenate([jnp.cos(angle), jnp.cos(angle)], axis=1)
    sine = jnp.concatenate([-jnp.sin(angle), jnp.sin(angle)], axis=1)

    resident = resident_kv[0, 0]
    keyval_shift = keyval_bias[0]
    swap = [(0, 1), (1, 0)]
    relay = [(i, i + 1) for i in range(section_count - 1)]

    dest_count = roll_count * section_count
    slots = block_table.shape[2]
    routing = block_table.reshape(dest_count, slots, 2)
    targets = routing[:, :, 0]
    slot_ids = routing[:, :, 1]
    own = rollout * section_count + section

    def order_of(device):
        return device % section_count * roll_count + device // section_count

    sources = jnp.arange(dest_count, dtype=jnp.int32)
    source_pages = (
        resumed_pages[:, None]
        + (section_count - 1 - jnp.arange(section_count, dtype=jnp.int32))[None, :]
        + BLOCKS
    )
    live_pages = jnp.where(section_active[None, :] > 0, source_pages, 0).reshape(-1)
    page_ids = jnp.arange(slots, dtype=jnp.int32)
    mine = (targets == own) & (page_ids[None, :] < live_pages[:, None])
    hit = mine[:, :, None] & (slot_ids[:, :, None] == page_ids)
    origin = jnp.max(jnp.where(hit, order_of(sources)[:, None, None], -1), axis=(0, 1))

    def table_of(block_table):
        slots_of = order_of(block_table.reshape(dest_count, slots, 2)[own, :, 0])
        return jnp.concatenate([slots_of, (length // PAGE)[None]]).astype(jnp.int32)


    heads = kv_width // HD
    pages = resident.reshape(-1, 2, heads, HD).swapaxes(1, 2).reshape(-1, PAGE * 2 * heads, HD)

    fresh_keys = []
    fresh_vals = []
    fresh = []
    results = []
    for step in range(BLOCKS):
        last = step == BLOCKS - 1
        if step == 0:
            inputs = [entering[0], lax.ppermute(entering[0], "tensor", swap)]
        else:
            handed = lax.ppermute(results[-1], "section", relay)
            if step == 1:
                slots_ahead, _ = lax.optimization_barrier((early[-1], results[-1]))
                outgoing = ship(slots_ahead, pages, dest_count)
                handed, outgoing = lax.optimization_barrier((handed, outgoing))
            inputs = [handed, lax.ppermute(handed, "tensor", swap)]
            inputs += early[2 * step - 2 : 2 * step]
        outs = project((2,), where, inputs, norm_gain, wq, wkv)
        outs.update(project((1, 3, 0), where, inputs, norm_gain, wq, wkv))
        if step == 0:
            late, given, table, outs[0] = lax.optimization_barrier(
                (resident, arriving, block_table, outs[0])
            )
            table = table_of(table)
            cache = late.reshape(resident.shape[0], 2 * kv_width)
            given_far = lax.ppermute(given, "tensor", swap)
            early = [given[0], given_far[0], given[1], given_far[1], table]
        outs = combine(first_sum(outs))
        if step == 0:
            outs, early = lax.optimization_barrier((outs, early))
        parts = [outs[0]] + [ring(outs[d], SECOND, d) for d in (2, 1, 3)]
        at = slice(step * BLOCK, (step + 1) * BLOCK)
        if last:
            fresh.append(new_page(parts, cosine[at], sine[at], keyval_shift))
            outgoing = ship_last(early[-1], fresh, outgoing)
            arrived = lax.all_to_all(outgoing, ("section",) + ROLL, 0, 0, tiled=True)
            pool = store(origin, arrived, slots)
        olds = []
        if fresh_keys:
            olds = [jnp.concatenate(fresh_keys), jnp.concatenate(fresh_vals)]
        attended, key, val, page = attend(
            length[None],
            parts,
            cosine[at],
            sine[at],
            query_bias,
            keyval_shift,
            cache,
            olds,
        )
        fresh_keys.append(key)
        fresh_vals.append(val)
        fresh.append(page)
        ahead, across, behind = [ring(attended, FIRST, SIDE - d) for d in range(1, SIDE)]
        gathered = join([attended, ahead, across, behind])
        gathered = gate(gathered, lax.ppermute(gathered[:16, :HD], "tensor", swap))
        late_mix = w_mix
        blocks = [gathered] + [ring(gathered, SECOND, SIDE - d) for d in range(1, SIDE)]
        if last:
            late_mix, pool = lax.optimization_barrier((w_mix, pool))
        mine, other = place(where, [dot(block, late_mix).astype(BF16) for block in blocks])
        theirs = lax.ppermute(other, "tensor", swap)
        kept = inputs[::2]
        results.append(merge(where, section_active, mine, theirs, kept, results if last else ()))
    section_out = results[-1][None]

    pool = pool.reshape(slots * PAGE, heads, 2, HD).swapaxes(1, 2)
    return section_out, pool.reshape(1, 1, slots, PAGE, 2, kv_width)


def solution(mesh):
    split = Mesh(mesh.devices.reshape(SIDE, SIDE, mesh.shape["section"], 2), ALL)
    in_specs = (
        P("section", "tensor", ROLL),
        P(None, "tensor", ROLL),
        P("section", ROLL, "tensor"),
        P("section", ROLL, None, "tensor"),
        P("section", "tensor", ROLL),
        P("section", "tensor"),
        P("section", None, "tensor"),
        P("section", ROLL),
        P(ROLL, "section", None, None, "tensor"),
        P(),
        P(),
        P(),
    )
    out_specs = (
        P("section", None, "tensor", ROLL),
        P(ROLL, "section", None, None, None, "tensor"),
    )
    return jax.shard_map(
        local, mesh=split, in_specs=in_specs, out_specs=out_specs, check_vma=False
    )
```
